128 devices in a mesh: ctx: 8 (over z, x_lo), tp: 4 (over x_hi, core), grp: 4 (over y).
Axes of the slice: x: 4 (x_hi: 2, x_lo: 2; x = x_hi * 2 + x_lo), y: 4, z: 4, core: 2. Of those that a mesh axis runs over, the one named last changes fastest.
Arguments:
- prompt_ids: int32 [16384], P(('grp', 'ctx')), parts along dimension 0, may hold values from 0 to 38015, as said below
- first_ids: int32 [64], P(('grp', 'ctx')), parts along dimension 0, may hold values from 0 to 38015
- table: bfloat16 [38016, 5120], P('ctx', 'tp'), may hold values from -6 to 6
- norm_gain: float32 [5120], replicated, may hold values from 0.1 to 1.9
- slot_map: int32 [16], replicated, may hold values from 0 to 15, each once
- w_query: bfloat16 [16, 320, 5120], P('ctx', None, 'tp'), may hold values from -0.078125 to 0.078125
- key_weight: bfloat16 [16, 320, 1024], P('ctx', None, 'tp'), may hold values from -0.078125 to 0.078125
- value_weight: bfloat16 [16, 320, 1024], P('ctx', None, 'tp'), may hold values from -0.078125 to 0.078125
- b_query: float32 [5120], P('tp'), may hold values from -7 to 7
- b_key: float32 [1024], P('tp'), may hold values from -7 to 7
- value_bias: float32 [1024], P('tp'), may hold values from -3 to 3
Outputs:
- prompt_heads: bfloat16 [16384, 5120], P(('grp', 'ctx'), 'tp'), parts along dimension 0
- sample_heads: bfloat16 [64, 5120], P(('grp', 'ctx'), 'tp'), parts along dimension 0
The draws below stay inside these ranges and needn't reach their ends.
There are 4 independent parts, one for each index of `grp`. The reference program is written for one: setup_inputs(seed, part) draws one part's arguments, and reference() takes and returns one part's arrays. A program takes and returns all parts, laid end to end along the dimension named above; an argument that names none is the same for every part. Nothing has to cross between parts.
Inputs may be any that keep to these rules, and one draw needn't show every extreme that they name: `slot_map`: each slot of 0 to 15 is named by exactly one bucket. `prompt_ids`: of the 512 prompt positions of one index of ctx, at most 128 have ids in any one block of 4752 ids (o * 4752 to (o + 1) * 4752 - 1); in every group some such block holds exactly 128 of the positions of every index of ctx.
All inputs are finite; a program needn't handle non-finite values.
Results may differ from the reference program's by a relative error of at most 0.01.
The reference program's roundings to bfloat16 on the way count: a program that leaves them out, or rounds other values in their place, can miss the bound.
Values may be sent and summed in bfloat16 or wider, within the bound.
No kernel may reach another device: no remote copies, remote signals or barrier semaphores. Data moves between devices by JAX's collectives and lax.ppermute only.
A program may use at most 256 MiB of HBM per device.

```python
import math
import jax
import jax.numpy as jnp
import numpy as np
from jax import lax

MODEL_WIDTH = 5120
QUERY_HEADS = 40
KEY_VALUE_HEADS = 8
HEAD_SIZE = 128
VOCAB_DEV = 4752
TOK_DEV = 512
VOCAB = 38016
PROMPT = 4096
GROUP_SAMPLES = 16
WEIGHT_BUCKETS = 16
TOK_CAP = 128


def shared_pattern(key):
    picked_entries = jax.random.permutation(jax.random.fold_in(key, 901), KEY_VALUE_HEADS)
    chosen_rows = picked_entries[:max(1, KEY_VALUE_HEADS // 4)]
    marked_entries = jnp.any(jnp.arange(KEY_VALUE_HEADS, dtype=jnp.int32)[:, None] == chosen_rows[None, :], axis=1)
    sign_values = jnp.where(jax.random.bernoulli(jax.random.fold_in(key, 902), 0.5, (KEY_VALUE_HEADS, HEAD_SIZE)), 1.0, -1.0)
    slow = jnp.arange(HEAD_SIZE, dtype=jnp.int32) % (HEAD_SIZE // 2) >= HEAD_SIZE // 4
    return jnp.where(marked_entries[:, None] & slow[None, :], sign_values, 0.0).astype(jnp.float32)


def draw_b_key(key, part):
    mask_pattern = shared_pattern(key)
    key = jax.random.fold_in(key, 21)
    signal_strength = 6.5
    rotary_base = jnp.clip(0.5 * jax.random.normal(key, (KEY_VALUE_HEADS, HEAD_SIZE), jnp.float32), -3.0, 3.0)
    return jnp.where(mask_pattern != 0.0, signal_strength * mask_pattern, rotary_base).reshape(KEY_VALUE_HEADS * HEAD_SIZE)


def draw_b_query(key, part):
    mask_pattern = shared_pattern(key)
    key = jax.random.fold_in(key, 22)
    group_members = QUERY_HEADS // KEY_VALUE_HEADS
    factors = 1.0 - 0.4 * jnp.arange(group_members, dtype=jnp.float32) / max(group_members - 1, 1)
    expanded = mask_pattern[:, None, :] * factors[None, :, None]
    signal_strength = 6.5
    rotary_base = jnp.clip(0.5 * jax.random.normal(key, (KEY_VALUE_HEADS, group_members, HEAD_SIZE), jnp.float32), -3.0, 3.0)
    return jnp.where(expanded != 0.0, signal_strength * expanded, rotary_base).reshape(QUERY_HEADS * HEAD_SIZE)


def draw_prompt_ids(key, part):
    key = jax.random.fold_in(key, 5)
    block_list = PROMPT // TOK_DEV
    owners = VOCAB // VOCAB_DEV
    rest = TOK_DEV - TOK_CAP
    keys = jax.random.split(key, 6)
    full_owner = jax.random.randint(keys[0], (), 0, owners).astype(jnp.int32)

    def one_block(block_key):
        first_key, second_key = jax.random.split(block_key)
        slots = jax.random.permutation(first_key, (owners - 1) * TOK_CAP)[:rest].astype(jnp.int32)
        others = (full_owner + 1 + slots // TOK_CAP) % owners
        chosen_rows = jnp.concatenate([jnp.full((TOK_CAP,), full_owner, jnp.int32), others.astype(jnp.int32)])
        return jax.random.permutation(second_key, chosen_rows)
    owner_of = jax.vmap(one_block)(jax.random.split(keys[1], block_list)).astype(jnp.int32)
    first_draw = jax.random.randint(keys[2], (block_list, TOK_DEV), 0, VOCAB_DEV)
    second_draw = jax.random.randint(keys[3], (block_list, TOK_DEV), 0, VOCAB_DEV)
    third_draw = jax.random.randint(keys[4], (block_list, TOK_DEV), 0, VOCAB_DEV)
    lowest = jnp.minimum(first_draw, jnp.minimum(second_draw, third_draw))
    shifts = jax.random.randint(keys[5], (owners,), 0, VOCAB_DEV)
    offset = (lowest + shifts[owner_of]) % VOCAB_DEV
    return (owner_of * VOCAB_DEV + offset).astype(jnp.int32).reshape(PROMPT)


def plant(values, own_key, least, top_value):
    shape = values.shape
    spot = [jax.random.randint(jax.random.fold_in(own_key, axis), (), 0, shape[axis]) for axis in range(len(shape))]
    values = values.at[tuple(spot)].set(least)
    longest = shape.index(max(shape))
    spot[longest] = (spot[longest] + 1) % shape[longest]
    return values.at[tuple(spot)].set(top_value)


def steps_of(own_key, extent, shards, low, largest):
    def one(dim, parts):
        heights = jax.random.uniform(jax.random.fold_in(jax.random.fold_in(own_key, 6), dim), (parts,), jnp.float32, low / len(shards), largest / len(shards))
        return jnp.repeat(jnp.exp(heights), extent[dim] // parts).reshape((-1,) + (1,) * (len(extent) - dim - 1))

    level = one(*shards[0])
    for cut in shards[1:]:
        level = level * one(*cut)
    return level


def rank_table(count, skew):
    loads = [(1 << 20) // math.isqrt(grade ** skew) + 1 for grade in range(1, count + 1)]
    scale = 1 + sum(loads) // (1 << 30)
    return np.cumsum(np.array([max(1, weight // scale) for weight in loads]))


def ranked(stream_key, shape, number_of, slope):
    table = rank_table(number_of, slope)
    ticket = jax.random.randint(jax.random.fold_in(stream_key, 1), shape, 0, int(table[number_of - 1]))
    standing = jnp.searchsorted(jnp.asarray(table, jnp.int32), ticket, side="right")
    return jax.random.permutation(jax.random.fold_in(stream_key, 2), number_of)[standing].astype(jnp.int32)


def normal_values(stream_key, extent, deviation, limit, shards=(), held_as=jnp.bfloat16):
    values = deviation * jax.random.normal(stream_key, extent, jnp.float32)
    if shards:
        values = values * steps_of(stream_key, extent, shards, -0.22, 0.18)
    return jnp.clip(values, -limit, limit).astype(held_as)


def setup_inputs(seed: int = 0, part: int = 0) -> dict:
    key_of = jax.random.split(jax.random.key(seed), 12)
    part_splits = jax.random.split(jax.random.fold_in(key_of[11], part), 12)
    prompt_ids = draw_prompt_ids(jax.random.fold_in(jax.random.fold_in(key_of[11], part), 71), part)
    first_ids = plant(ranked(part_splits[1], (GROUP_SAMPLES,), VOCAB, 2), jax.random.fold_in(part_splits[1], 3), 0, VOCAB - 1).astype(jnp.int32)
    table = normal_values(key_of[2], (VOCAB, MODEL_WIDTH), 1.0, 6.0, ((0, 8), (1, 4)))
    norm_gain = jnp.clip(1.0 + 0.18 * jax.random.normal(key_of[3], (MODEL_WIDTH,), jnp.float32), 0.1, 1.9)
    slot_map = jax.random.permutation(key_of[4], WEIGHT_BUCKETS).astype(jnp.int32)
    w_query = normal_values(key_of[5], (WEIGHT_BUCKETS, MODEL_WIDTH // WEIGHT_BUCKETS, QUERY_HEADS * HEAD_SIZE), MODEL_WIDTH ** -0.5, 0.078125, ((0, 8), (2, 4)))
    key_weight = normal_values(key_of[6], (WEIGHT_BUCKETS, MODEL_WIDTH // WEIGHT_BUCKETS, KEY_VALUE_HEADS * HEAD_SIZE), MODEL_WIDTH ** -0.5, 0.078125, ((0, 8), (2, 4)))
    value_weight = normal_values(key_of[7], (WEIGHT_BUCKETS, MODEL_WIDTH // WEIGHT_BUCKETS, KEY_VALUE_HEADS * HEAD_SIZE), MODEL_WIDTH ** -0.5, 0.078125, ((0, 8), (2, 4)))
    b_query = draw_b_query(jax.random.fold_in(key_of[11], 71), part)
    b_key = draw_b_key(jax.random.fold_in(key_of[11], 71), part)
    value_bias = normal_values(key_of[10], (KEY_VALUE_HEADS * HEAD_SIZE,), 0.5, 3.0, ((0, 4),), jnp.float32)
    return dict(prompt_ids=prompt_ids, first_ids=first_ids, table=table, norm_gain=norm_gain, slot_map=slot_map, w_query=w_query, key_weight=key_weight, value_weight=value_weight, b_query=b_query, b_key=b_key, value_bias=value_bias)


EPS = 1e-06
THETA = 1000000.0

def apply_rotation(tensor, token_positions):
    width = tensor.shape[-1]
    half_width = width // 2
    frequency = jnp.power(THETA, -jnp.arange(half_width, dtype=jnp.float32) * 2.0 / width)
    angles = token_positions.astype(jnp.float32)[:, None] * frequency[None, :]
    cosine = jnp.cos(angles)[:, None, :]
    sine_part = jnp.sin(angles)[:, None, :]
    lower_half = tensor[..., :half_width]
    upper_half = tensor[..., half_width:]
    return jnp.concatenate([lower_half * cosine - upper_half * sine_part, upper_half * cosine + lower_half * sine_part], axis=-1)

def reference(prompt_ids, first_ids, table, norm_gain, slot_map, w_query, key_weight, value_weight, b_query, b_key, value_bias):
    group_members = QUERY_HEADS // KEY_VALUE_HEADS
    scale = 1.0 / math.sqrt(HEAD_SIZE)

    def normalize(token_ids):
        looked = table[token_ids].astype(jnp.float32)
        factor = lax.rsqrt(lax.optimization_barrier(jnp.mean(looked * looked, axis=-1, keepdims=True)) + EPS)
        return (looked * factor * norm_gain).astype(jnp.bfloat16)

    def unbucket(weight):
        return jnp.zeros(weight.shape, weight.dtype).at[slot_map].set(weight).reshape(MODEL_WIDTH, weight.shape[2])
    big_q = unbucket(w_query)
    big_k = unbucket(key_weight)
    big_v = unbucket(value_weight)

    def project(normed, token_positions):
        query = jnp.dot(normed, big_q, preferred_element_type=jnp.float32) + b_query
        query = apply_rotation(query.reshape(-1, QUERY_HEADS, HEAD_SIZE), token_positions).astype(jnp.bfloat16)
        key_portion = jnp.dot(normed, big_k, preferred_element_type=jnp.float32) + b_key
        key_portion = apply_rotation(key_portion.reshape(-1, KEY_VALUE_HEADS, HEAD_SIZE), token_positions).astype(jnp.bfloat16)
        value_portion = jnp.dot(normed, big_v, preferred_element_type=jnp.float32) + value_bias
        value_portion = value_portion.reshape(-1, KEY_VALUE_HEADS, HEAD_SIZE).astype(jnp.bfloat16)
        return (query, key_portion, value_portion)
    prompt_pos = jnp.arange(PROMPT, dtype=jnp.int32)
    prompt_q, prompt_k, prompt_v = project(normalize(prompt_ids), prompt_pos)
    sample_query_rows, sample_k, sample_v = project(normalize(first_ids), jnp.full((GROUP_SAMPLES,), PROMPT, jnp.int32))
    causal = prompt_pos[:, None] >= prompt_pos[None, :]

    def block_of_heads(head_index):
        query_rows = lax.dynamic_slice_in_dim(prompt_q, head_index * group_members, group_members, 1).astype(jnp.float32)
        key_rows = lax.dynamic_index_in_dim(prompt_k, head_index, 1, keepdims=False).astype(jnp.float32)
        value_rows = lax.dynamic_index_in_dim(prompt_v, head_index, 1, keepdims=False).astype(jnp.float32)
        scores = jnp.einsum('qed,kd->eqk', query_rows, key_rows) * scale
        scores = jnp.where(causal[None], scores, -jnp.inf)
        row_max = lax.optimization_barrier(jnp.max(scores, axis=-1, keepdims=True))
        expo = jnp.exp(scores - row_max)
        denom = lax.optimization_barrier(jnp.sum(expo, axis=-1))
        probs = lax.optimization_barrier(expo.astype(jnp.bfloat16)).astype(jnp.float32)
        return jnp.einsum('eqk,kd->qed', probs, value_rows) / jnp.transpose(denom)[:, :, None]
    block_list = lax.map(block_of_heads, jnp.arange(KEY_VALUE_HEADS, dtype=jnp.int32))
    prompt_heads = jnp.transpose(block_list, (1, 0, 2, 3)).reshape(PROMPT, QUERY_HEADS * HEAD_SIZE).astype(jnp.bfloat16)
    query_rows = sample_query_rows.reshape(GROUP_SAMPLES, KEY_VALUE_HEADS, group_members, HEAD_SIZE).astype(jnp.float32)
    cache_scores = jnp.einsum('sged,kgd->sgek', query_rows, prompt_k.astype(jnp.float32)) * scale
    own_scores = jnp.einsum('sged,sgd->sge', query_rows, sample_k.astype(jnp.float32)) * scale
    every_score = jnp.concatenate([cache_scores, own_scores[..., None]], axis=-1)
    row_max = lax.optimization_barrier(jnp.max(every_score, axis=-1, keepdims=True))
    expo = jnp.exp(every_score - row_max)
    denom = lax.optimization_barrier(jnp.sum(expo, axis=-1))
    probs = lax.optimization_barrier(expo.astype(jnp.bfloat16)).astype(jnp.float32)
    mixed = jnp.einsum('sgek,kgd->sged', probs[..., :PROMPT], prompt_v.astype(jnp.float32))
    mixed = mixed + probs[..., PROMPT][..., None] * sample_v.astype(jnp.float32)[:, :, None, :]
    sample_heads = (mixed / denom[..., None]).reshape(GROUP_SAMPLES, QUERY_HEADS * HEAD_SIZE).astype(jnp.bfloat16)
    return (prompt_heads, sample_heads)
```

```python
import functools
import math

import jax
import jax.numpy as jnp
from jax import lax
from jax.experimental import pallas as pl
from jax.experimental.pallas import tpu as pltpu
from jax.sharding import PartitionSpec as P

HEAD = 128
EPS = 1e-06
THETA = 1000000.0
NEG = -1e30
AXES = ("ctx", "tp", "grp")
CAP = 128
MSG = 136
ROWS = 528
TOK = 512
SIZE = 4
VMEM = 56 * 1024 * 1024
DEEP = 1280
FAR_Z = (3, 1, 2)


def device_number(x, y, z, core):
    return ((z * 2 + x % 2) * 4 + (x // 2) * 2 + core) * 4 + y


def move(array, dx=0, dy=0, dz=0, pair=0, core=0):
    pairs = []
    for x in range(SIZE):
        for y in range(SIZE):
            for z in range(SIZE):
                for c in range(2):
                    there = ((x + dx) % SIZE) ^ pair, (y + dy) % SIZE, (z + dz) % SIZE, c ^ core
                    pairs.append((device_number(x, y, z, c), device_number(*there)))
    return lax.ppermute(array, AXES, pairs)


def rope_tables(positions):
    half = HEAD // 2
    frequency = jnp.power(THETA, -jnp.arange(half, dtype=jnp.float32) * 2.0 / HEAD)
    angles = positions.astype(jnp.float32)[:, None] * frequency[None, :]
    cosine, sine = jnp.cos(angles), jnp.sin(angles)
    return jnp.concatenate([cosine, cosine], 1), jnp.concatenate([-sine, sine], 1)


def rotate(value, cosine, sine):
    return value * cosine + pltpu.roll(value, HEAD // 2, 1) * sine


def weight_copies(meta, slots, own, near, far, held, sems, low, width):
    z, y, j = meta[1], meta[2], meta[3]
    copies = []

    def one(ref, bucket):
        copies.append(
            pltpu.make_async_copy(
                ref.at[:, pl.ds(low, width)], held.at[slots[bucket]], sems.at[len(copies)]
            )
        )

    for i in range(2):
        one(own.at[i], 4 * z + 2 * j + i)
    one(near[0], 4 * z + 2 * (1 - j) + lax.rem(y, 2))
    one(near[1], 4 * z + 2 * (1 - j) + 1 - lax.rem(y, 2))
    for other_y in range(SIZE):
        for index, dz in enumerate(FAR_Z):
            one(far.at[other_y, index], 4 * lax.rem(z + dz, SIZE) + other_y)
    for copy in copies:
        copy.start()
    return copies


def kv_kernel(piece_at, meta, slots, *refs):
    n_piece = len(piece_at)
    pieces = refs[:n_piece]
    own, near0, near1, far, gain, cosine, sine, b_key, b_value = refs[n_piece : n_piece + 9]
    kv_out, normed_out, rows, held, acc, row_sems, held_sems, out_sem = refs[n_piece + 9 :]
    x, core = meta[0], meta[4]
    copies = []
    for ref, (dx, other, start, count) in zip(pieces, piece_at):
        there = lax.rem(x + dx, SIZE)
        feature = 2 * (there // 2) + (1 - core if other else core)
        width = ref.shape[1]
        target = rows.at[
            lax.rem(there, 2),
            pl.ds(start, count),
            pl.ds(pl.multiple_of(feature * width, 128), width),
        ]
        copies.append(pltpu.make_async_copy(ref, target, row_sems.at[len(copies)]))
    for copy in copies:
        copy.start()
    weights = weight_copies(
        meta, slots, own, (near0, near1), far, held, held_sems, 5 * HEAD, 2 * HEAD
    )
    for copy in copies:
        copy.wait()
    step = 16

    def normalize(index, _):
        part = index // (ROWS // step)
        span = pl.ds(pl.multiple_of(lax.rem(index, ROWS // step) * step, step), step)
        values = rows[part, span, :].astype(jnp.float32)
        factor = lax.rsqrt(jnp.mean(values * values, axis=-1, keepdims=True) + EPS)
        rows[part, span, :] = (values * factor * gain[...]).astype(jnp.bfloat16)
        return 0

    lax.fori_loop(0, 2 * ROWS // step, normalize, 0)
    out = pltpu.make_async_copy(rows, normed_out, out_sem)
    out.start()
    for copy in weights:
        copy.wait()
    acc[...] = jnp.zeros_like(acc)

    def multiply(k, _):
        left = rows[:, :, pl.ds(pl.multiple_of(k * DEEP, 128), DEEP)].reshape(2 * ROWS, DEEP)
        right = held[pl.ds(4 * k, 4)].reshape(DEEP, 2 * HEAD)
        acc[...] += jnp.dot(left, right, preferred_element_type=jnp.float32)
        return 0

    lax.fori_loop(0, 4, multiply, 0)
    key = rotate(acc[:, :HEAD] + b_key[...], cosine[...], sine[...])
    value = acc[:, HEAD:] + b_value[...]
    kv_out[:, :, :HEAD] = key.astype(jnp.bfloat16).reshape(2, ROWS, HEAD)
    kv_out[:, :, HEAD:] = value.astype(jnp.bfloat16).reshape(2, ROWS, HEAD)
    out.wait()


def q_kernel(
    meta, slots, normed, own, near0, near1, far, cosine, sine, b_query, q_out,
    rows, held, acc, row_sems, held_sems,
):
    copies = []
    for k in range(4):
        span = pl.ds(k * DEEP, DEEP)
        copies.append(
            pltpu.make_async_copy(normed.at[:, :, span], rows.at[:, :, span], row_sems.at[k])
        )
    for copy in copies:
        copy.start()
    weights = weight_copies(meta, slots, own, (near0, near1), far, held, held_sems, 0, 5 * HEAD)
    for copy in weights:
        copy.wait()
    for copy in copies:
        copy.wait()
    acc[...] = jnp.zeros_like(acc)

    def multiply(k, _):
        left = rows[:, :, pl.ds(pl.multiple_of(k * DEEP, 128), DEEP)].reshape(2 * ROWS, DEEP)
        right = held[pl.ds(4 * k, 4)].reshape(DEEP, 5 * HEAD)
        acc[...] += jnp.dot(left, right, preferred_element_type=jnp.float32)
        return 0

    lax.fori_loop(0, 4, multiply, 0)
    for head in range(5):
        span = slice(head * HEAD, (head + 1) * HEAD)
        turned = rotate(acc[:, span] + b_query[:, span], cosine[...], sine[...])
        q_out[:, :, span] = turned.astype(jnp.bfloat16).reshape(2, ROWS, HEAD)


def project(meta, slots, pieces, piece_at, weights, gain, cosine, sine, b_q, b_k, b_v):
    smem = pl.BlockSpec(memory_space=pltpu.SMEM)
    vmem = pl.BlockSpec(memory_space=pltpu.VMEM)
    anywhere = pl.BlockSpec(memory_space=pl.ANY)
    width = 4 * DEEP
    kv, normed = pl.pallas_call(
        functools.partial(kv_kernel, piece_at),
        out_shape=(
            jax.ShapeDtypeStruct((2, ROWS, 2 * HEAD), jnp.bfloat16),
            jax.ShapeDtypeStruct((2, ROWS, width), jnp.bfloat16),
        ),
        in_specs=[smem, smem] + [anywhere] * (len(pieces) + 4) + [vmem] * 5,
        out_specs=(vmem, anywhere),
        scratch_shapes=[
            pltpu.VMEM((2, ROWS, width), jnp.bfloat16),
            pltpu.VMEM((16, 320, 2 * HEAD), jnp.bfloat16),
            pltpu.VMEM((2 * ROWS, 2 * HEAD), jnp.float32),
            pltpu.SemaphoreType.DMA((len(pieces),)),
            pltpu.SemaphoreType.DMA((16,)),
            pltpu.SemaphoreType.DMA,
        ],
        compiler_params=pltpu.CompilerParams(vmem_limit_bytes=VMEM),
        name="norm_kv",
    )(meta, slots, *pieces, *weights, gain, cosine, sine, b_k, b_v)
    query = pl.pallas_call(
        q_kernel,
        out_shape=jax.ShapeDtypeStruct((2, ROWS, 5 * HEAD), jnp.bfloat16),
        in_specs=[smem, smem] + [anywhere] * 5 + [vmem] * 3,
        out_specs=vmem,
        scratch_shapes=[
            pltpu.VMEM((2, ROWS, width), jnp.bfloat16),
            pltpu.VMEM((16, 320, 5 * HEAD), jnp.bfloat16),
            pltpu.VMEM((2 * ROWS, 5 * HEAD), jnp.float32),
            pltpu.SemaphoreType.DMA((4,)),
            pltpu.SemaphoreType.DMA((16,)),
        ],
        compiler_params=pltpu.CompilerParams(vmem_limit_bytes=VMEM),
        name="query",
    )(meta, slots, normed, *weights, cosine, sine, b_q)
    return query, kv


def attend_kernel(meta, q, kv0, kv1, kv2, kv3, out, top, total, mixed):
    z, chunk = meta[0], meta[1]
    head = pl.program_id(0)
    pieces = (kv0, kv1, kv2, kv3)
    factor = math.log2(math.e) / math.sqrt(HEAD)
    span = pl.ds(pl.multiple_of(head * HEAD, HEAD), HEAD)
    block = 256

    def scores_of(query, keys):
        return lax.dot_general(
            query, keys, (((1,), (1,)), ((), ())), preferred_element_type=jnp.float32
        )

    for part in range(TOK // block):
        span_rows = pl.ds(part * block, block)
        query = q[0, span_rows, span]
        top[...] = jnp.full_like(top, NEG)
        total[...] = jnp.zeros_like(total)
        mixed[...] = jnp.zeros_like(mixed)

        def fold(ref, half, masked):
            keys = ref[half, :TOK, :HEAD]
            values = ref[half, :TOK, HEAD:]
            scores = scores_of(query, keys)
            if masked:
                row = part * block + lax.broadcasted_iota(jnp.int32, scores.shape, 0)
                column = lax.broadcasted_iota(jnp.int32, scores.shape, 1)
                scores = jnp.where(column <= row, scores, NEG)
            before = top[...]
            now = jnp.maximum(before, jnp.max(scores, axis=-1, keepdims=True))
            expo = jnp.exp2((scores - now) * factor)
            scale = jnp.exp2((before - now) * factor)
            top[...] = now
            total[...] = total[...] * scale + jnp.sum(expo, axis=-1, keepdims=True)
            mixed[...] = mixed[...] * scale + jnp.dot(
                expo.astype(jnp.bfloat16), values, preferred_element_type=jnp.float32
            )

        @pl.when(chunk == 0)
        def _():
            fold(kv0, 0, True)

        @pl.when(chunk == 1)
        def _():
            fold(kv0, 0, False)
            fold(kv0, 1, True)

        for away in range(1, SIZE):

            @pl.when(z >= away)
            def _():
                fold(pieces[away], 0, False)
                fold(pieces[away], 1, False)

        out[span_rows, span] = (mixed[...] / total[...]).astype(jnp.bfloat16)

    @pl.when(head == 4)
    def _():
        tail = ROWS - TOK
        query = jnp.concatenate(
            [q[0, TOK:, g * HEAD : (g + 1) * HEAD] for g in range(5)], axis=0
        )
        own_key = kv0[chunk, TOK:, :HEAD].astype(jnp.float32)
        own_value = kv0[chunk, TOK:, HEAD:].astype(jnp.float32)
        own = jnp.sum(
            query.astype(jnp.float32) * jnp.concatenate([own_key] * 5, axis=0),
            axis=-1,
            keepdims=True,
        )
        every = [
            scores_of(query, ref[half, :TOK, :HEAD]) for ref in pieces for half in range(2)
        ]
        peak = own
        for scores in every:
            peak = jnp.maximum(peak, jnp.max(scores, axis=-1, keepdims=True))
        expo = jnp.exp2((own - peak) * factor)
        weight = expo
        summed = expo.astype(jnp.bfloat16).astype(jnp.float32) * jnp.concatenate(
            [own_value] * 5, axis=0
        )
        for index, scores in enumerate(every):
            expo = jnp.exp2((scores - peak) * factor)
            weight = weight + jnp.sum(expo, axis=-1, keepdims=True)
            summed = summed + jnp.dot(
                expo.astype(jnp.bfloat16),
                pieces[index // 2][index % 2, :TOK, HEAD:],
                preferred_element_type=jnp.float32,
            )
        done = (summed / weight).astype(jnp.bfloat16)
        for g in range(5):
            out[TOK:, g * HEAD : (g + 1) * HEAD] = done[g * tail : (g + 1) * tail]


def attend(z, chunk, query, kvs):
    return pl.pallas_call(
        attend_kernel,
        out_shape=jax.ShapeDtypeStruct((ROWS, 5 * HEAD), jnp.bfloat16),
        grid_spec=pltpu.PrefetchScalarGridSpec(
            num_scalar_prefetch=1,
            grid=(5,),
            in_specs=[pl.BlockSpec((1, ROWS, 5 * HEAD), lambda g, meta: (meta[1], 0, 0))]
            + [pl.BlockSpec((2, ROWS, 2 * HEAD), lambda g, meta: (0, 0, 0))] * 4,
            out_specs=pl.BlockSpec((ROWS, 5 * HEAD), lambda g, meta: (0, 0)),
            scratch_shapes=[
                pltpu.VMEM((256, 1), jnp.float32),
                pltpu.VMEM((256, 1), jnp.float32),
                pltpu.VMEM((256, HEAD), jnp.float32),
            ],
        ),
        compiler_params=pltpu.CompilerParams(vmem_limit_bytes=VMEM),
        name="attend",
    )(jnp.stack([z, chunk]).astype(jnp.int32), query, *kvs)


def counts_before(flags):
    upto = jnp.arange(TOK)[:, None] <= jnp.arange(TOK)[None, :]
    return jnp.dot(
        flags.astype(jnp.bfloat16), upto.astype(jnp.bfloat16), preferred_element_type=jnp.float32
    ).astype(jnp.int32)


def local(
    prompt_ids,
    first_ids,
    table,
    norm_gain,
    slot_map,
    w_query,
    key_weight,
    value_weight,
    b_query,
    b_key,
    value_bias,
):
    ctx = lax.axis_index("ctx")
    tp = lax.axis_index("tp")
    y = lax.axis_index("grp")
    z, j = ctx // 2, ctx % 2
    x, core = (tp // 2) * 2 + j, tp % 2
    vocab_dev, features = table.shape
    samples = first_ids.shape[0]

    def columns(head):
        pick = lambda w, n: lax.dynamic_slice_in_dim(w, head * n, n, 2)
        return jnp.concatenate(
            [pick(w_query, 5 * HEAD), pick(key_weight, HEAD), pick(value_weight, HEAD)], axis=2
        )

    own = columns(j)
    give = columns(1 - j)
    first = y % 2
    near0 = move(lax.dynamic_index_in_dim(give, first, 0, keepdims=False), pair=1)
    near1 = move(lax.dynamic_index_in_dim(give, 1 - first, 0, keepdims=False), pair=1)

    mine = jnp.concatenate([prompt_ids, first_ids])[None]
    both = jnp.concatenate([mine, move(mine, pair=1)], axis=0)
    ids = jnp.concatenate([both, move(both, dz=-1), move(both, dz=2), move(both, dz=1)], axis=0)

    wanted = ids - ctx * vocab_dev
    inside = (wanted >= 0) & (wanted < vocab_dev)
    rank = jnp.where(inside[:, :TOK], counts_before(inside[:, :TOK]) - 1, -1)
    at_slot = rank[:, None, :] == jnp.arange(CAP, dtype=jnp.int32)[None, :, None]
    chosen = jnp.sum(jnp.where(at_slot, wanted[:, None, :TOK], 0), axis=-1)
    chosen = jnp.concatenate(
        [
            chosen,
            jnp.where(inside[:, TOK:], wanted[:, TOK:], 0),
            jnp.zeros((8, MSG - CAP - samples), jnp.int32),
        ],
        axis=1,
    )
    messages = [
        table.at[chosen[n]].get(mode="promise_in_bounds") for n in range(2 * SIZE)
    ]
    arrived = [
        message if n == 0 else move(message, dz=n // 2, pair=n % 2)
        for n, message in enumerate(messages)
    ]
    arrived = jnp.concatenate(arrived, axis=0)

    owner = mine[0] // vocab_dev
    counted = counts_before(
        owner[None, :TOK] == jnp.arange(2 * SIZE, dtype=jnp.int32)[:, None]
    )
    held_by = owner[None, :TOK] == jnp.arange(2 * SIZE, dtype=jnp.int32)[:, None]
    place = jnp.sum(jnp.where(held_by, counted - 1, 0), axis=0)
    place = jnp.concatenate([place, CAP + jnp.arange(samples, dtype=jnp.int32)])
    message_of = ((z - owner // 2) % SIZE) * 2 + (owner + ctx) % 2
    place = place + message_of * MSG
    place = jnp.concatenate([place, jnp.full((ROWS - TOK - samples,), -1, jnp.int32)])
    spread = place[:, None] == jnp.arange(2 * SIZE * MSG, dtype=jnp.int32)[None, :]
    embedded = jnp.dot(
        spread.astype(jnp.bfloat16), arrived, preferred_element_type=jnp.float32
    ).astype(jnp.bfloat16)

    half = 256
    left = move(embedded, dx=1)
    right = move(embedded, dx=-1)
    across0 = move(left[:half], dx=1)
    across1 = move(right[half:], dx=-1)
    pieces, piece_at = [], []
    for piece, dx, start in (
        (embedded, 0, 0),
        (left, 3, 0),
        (right, 1, 0),
        (across0, 2, 0),
        (across1, 2, half),
    ):
        pieces += [piece, move(piece, core=1)]
        piece_at += [(dx, other, start, piece.shape[0]) for other in (False, True)]

    part = jnp.where(j == y // 2, lax.dynamic_index_in_dim(own, first, 0, keepdims=False), near0)
    over_z = jnp.stack([move(part, dz=-dz) for dz in FAR_Z])
    far = lax.all_gather(over_z, "grp", axis=0, tiled=False)

    positions = jnp.arange(2 * ROWS, dtype=jnp.int32)
    chunk_of, row_of = positions // ROWS, positions % ROWS
    positions = jnp.where(
        row_of < TOK, z * 2 * TOK + chunk_of * TOK + row_of, SIZE * 2 * TOK
    )
    cosine, sine = rope_tables(positions)

    meta = jnp.stack([x, z, y, j, core]).astype(jnp.int32)
    take = lambda vector, n: lax.dynamic_slice_in_dim(vector, j * n, n, 0)[None]
    query, kv = project(
        meta,
        slot_map,
        pieces,
        piece_at,
        (own, near0, near1, far),
        norm_gain[None],
        cosine,
        sine,
        take(b_query, 5 * HEAD),
        take(b_key, HEAD),
        take(value_bias, HEAD),
    )
    kvs = [kv] + [move(kv, dz=dz) for dz in (1, 2, 3)]
    theirs = move(attend(z, 1 - j, query, kvs), pair=1)
    ours = attend(z, j, query, kvs)
    heads = jnp.where(
        j == 0,
        jnp.concatenate([ours, theirs], axis=1),
        jnp.concatenate([theirs, ours], axis=1),
    )
    return heads[:TOK], heads[TOK : TOK + samples]


def solution(mesh):
    placed = (
        P(("grp", "ctx")),
        P(("grp", "ctx")),
        P("ctx", "tp"),
        P(),
        P(),
        P("ctx", None, "tp"),
        P("ctx", None, "tp"),
        P("ctx", None, "tp"),
        P("tp"),
        P("tp"),
        P("tp"),
    )
    return jax.shard_map(
        local,
        mesh=mesh,
        in_specs=placed,
        out_specs=(P(("grp", "ctx"), "tp"), P(("grp", "ctx"), "tp")),
        check_vma=False,
    )
```

```python
import functools
import math

import jax
import jax.numpy as jnp
from jax import lax
from jax.experimental import pallas as pl
from jax.experimental.pallas import tpu as pltpu
from jax.sharding import PartitionSpec as P

HEAD = 128
EPS = 1e-06
THETA = 1000000.0
NEG = -1e30
AXES = ("ctx", "tp", "grp")
CAP = 128
MSG = 144
ROWS = 528
TOK = 512
SIZE = 4
VMEM = 56 * 1024 * 1024
DEEP = 1280
CUT = 256
WIDE = 256
WIDE = 256
FAR_Z = (3, 1, 2)


def device_number(x, y, z, core):
    return ((z * 2 + x % 2) * 4 + (x // 2) * 2 + core) * 4 + y


def move(array, dx=0, dy=0, dz=0, pair=0, core=0, side=0):
    pairs = []
    for x in range(SIZE):
        for y in range(SIZE):
            for z in range(SIZE):
                for c in range(2):
                    along = (x + dx + side * (2 * (x % 2) - 1)) % SIZE
                    there = along ^ pair, (y + dy) % SIZE, (z + dz) % SIZE, c ^ core
                    pairs.append((device_number(x, y, z, c), device_number(*there)))
    return lax.ppermute(array, AXES, pairs)


def rope_tables(positions):
    half = HEAD // 2
    frequency = jnp.power(THETA, -jnp.arange(half, dtype=jnp.float32) * 2.0 / HEAD)
    angles = positions.astype(jnp.float32)[:, None] * frequency[None, :]
    cosine, sine = jnp.cos(angles), jnp.sin(angles)
    return jnp.concatenate([cosine, cosine], 1), jnp.concatenate([-sine, sine], 1)


def rotate(value, cosine, sine):
    return value * cosine + pltpu.roll(value, HEAD // 2, 1) * sine


def weight_copies(slots, weights, held, sems):
    for bucket in range(16):
        slot = slots[bucket]
        pltpu.make_async_copy(weights.at[bucket], held.at[slot], sems.at[slot]).start()

    def wait(quarter):
        for slot in range(4 * quarter, 4 * quarter + 4):
            pltpu.make_async_copy(weights.at[0], held.at[slot], sems.at[slot]).wait()

    return wait


def kv_kernel(piece_at, meta, slots, *refs):
    n_piece = len(piece_at)
    pieces = refs[:n_piece]
    weights, gain, cosine, sine, b_key, b_value = refs[n_piece : n_piece + 6]
    kv_out, tail_out, normed_out, rows, held, acc, row_sems, held_sems, out_sem = refs[n_piece + 6 :]
    x, core = meta[0], meta[4]
    copies = []
    for ref, (dx, other, start, count) in zip(pieces, piece_at):
        there = lax.rem(x + dx, SIZE)
        feature = 2 * (there // 2) + (1 - core if other else core)
        width = ref.shape[1]
        target = rows.at[pl.ds(start, count), pl.ds(pl.multiple_of(feature * width, 128), width)]
        copies.append(pltpu.make_async_copy(ref, target, row_sems.at[len(copies)]))
    for copy in copies:
        copy.start()
    wait = weight_copies(slots, weights, held, held_sems)
    for copy in copies:
        copy.wait()
    step = 48
    lanes = [slice(low, low + HEAD) for low in range(0, rows.shape[1], HEAD)]

    def normalize(index, _):
        span = pl.ds(pl.multiple_of(index * step, 16), step)
        squares = jnp.zeros((step, HEAD), jnp.float32)
        for lane in lanes:
            values = rows[span, lane].astype(jnp.float32)
            squares = squares + values * values
        mean = jnp.sum(squares, axis=-1, keepdims=True) / rows.shape[1]
        factor = lax.rsqrt(mean + EPS)
        for lane in lanes:
            values = rows[span, lane].astype(jnp.float32)
            rows[span, lane] = (values * factor * gain[:, lane]).astype(jnp.bfloat16)
        return 0

    lax.fori_loop(0, ROWS // step, normalize, 0)
    out = pltpu.make_async_copy(rows, normed_out, out_sem)
    out.start()
    for k in range(4):
        wait(k)
        product = jnp.dot(
            rows[:, k * DEEP : (k + 1) * DEEP],
            held[4 * k : 4 * k + 4].reshape(DEEP, 2 * HEAD),
            preferred_element_type=jnp.float32,
        )
        acc[...] = product if k == 0 else acc[...] + product
    key = rotate(acc[:, :HEAD] + b_key[...], cosine[...], sine[...])
    value = acc[:, HEAD:] + b_value[...]
    kv_out[:TOK] = key[:TOK].astype(jnp.bfloat16)
    tail_out[0] = key[TOK:].astype(jnp.bfloat16)
    tail_out[1] = value[TOK:].astype(jnp.bfloat16)
    for start in range(0, TOK, HEAD):
        kv_out[TOK + start : TOK + start + HEAD] = (
            value[start : start + HEAD].T.astype(jnp.bfloat16)
        )
    out.wait()


def q_kernel(
    slots, normed, weights, cosine, sine, b_query, q_out, rows, held, acc, row_sems, held_sems,
):
    copies = []
    for k in range(4):
        span = pl.ds(k * DEEP, DEEP)
        copies.append(pltpu.make_async_copy(normed.at[:, span], rows.at[:, span], row_sems.at[k]))
    wait = weight_copies(slots, weights, held, held_sems)
    for copy in copies:
        copy.start()
    for k in range(4):
        wait(k)
        copies[k].wait()
        product = jnp.dot(
            rows[:, k * DEEP : (k + 1) * DEEP],
            held[4 * k : 4 * k + 4].reshape(DEEP, 5 * HEAD),
            preferred_element_type=jnp.float32,
        )
        acc[...] = product if k == 0 else acc[...] + product
    for head in range(5):
        span = slice(head * HEAD, (head + 1) * HEAD)
        turned = rotate(acc[:, span] + b_query[:, span], cosine[...], sine[...])
        q_out[:, span] = turned.astype(jnp.bfloat16)


SMEM_SPEC = pl.BlockSpec(memory_space=pltpu.SMEM)
VMEM_SPEC = pl.BlockSpec(memory_space=pltpu.VMEM)
ANY_SPEC = pl.BlockSpec(memory_space=pl.ANY)


def project_kv(meta, slots, pieces, weights, gain, cosine, sine, b_k, b_v):
    width = 4 * DEEP
    refs, piece_at = zip(*pieces)
    return pl.pallas_call(
        functools.partial(kv_kernel, piece_at),
        out_shape=(
            jax.ShapeDtypeStruct((2 * TOK, HEAD), jnp.bfloat16),
            jax.ShapeDtypeStruct((2, ROWS - TOK, HEAD), jnp.bfloat16),
            jax.ShapeDtypeStruct((ROWS, width), jnp.bfloat16),
        ),
        in_specs=[SMEM_SPEC] * 2 + [ANY_SPEC] * (len(refs) + 1) + [VMEM_SPEC] * 5,
        out_specs=(VMEM_SPEC, VMEM_SPEC, ANY_SPEC),
        scratch_shapes=[
            pltpu.VMEM((ROWS, width), jnp.bfloat16),
            pltpu.VMEM((16, 320, 2 * HEAD), jnp.bfloat16),
            pltpu.VMEM((ROWS, 2 * HEAD), jnp.float32),
            pltpu.SemaphoreType.DMA((len(refs),)),
            pltpu.SemaphoreType.DMA((16,)),
            pltpu.SemaphoreType.DMA,
        ],
        compiler_params=pltpu.CompilerParams(vmem_limit_bytes=VMEM),
        cost_estimate=pl.CostEstimate(
            flops=2 * ROWS * width * 2 * HEAD, bytes_accessed=30 * 2**20, transcendentals=0
        ),
        name="norm_kv",
    )(meta, slots, *refs, weights, gain, cosine, sine, b_k, b_v)


def project_q(slots, normed, weights, cosine, sine, b_q):
    width = 4 * DEEP
    return pl.pallas_call(
        q_kernel,
        out_shape=jax.ShapeDtypeStruct((ROWS, 5 * HEAD), jnp.bfloat16),
        in_specs=[SMEM_SPEC] + [ANY_SPEC] * 2 + [VMEM_SPEC] * 3,
        out_specs=VMEM_SPEC,
        scratch_shapes=[
            pltpu.VMEM((ROWS, width), jnp.bfloat16),
            pltpu.VMEM((16, 320, 5 * HEAD), jnp.bfloat16),
            pltpu.VMEM((ROWS, 5 * HEAD), jnp.float32),
            pltpu.SemaphoreType.DMA((4,)),
            pltpu.SemaphoreType.DMA((16,)),
        ],
        compiler_params=pltpu.CompilerParams(vmem_limit_bytes=VMEM),
        cost_estimate=pl.CostEstimate(
            flops=2 * ROWS * width * 5 * HEAD, bytes_accessed=24 * 2**20, transcendentals=0
        ),
        name="query",
    )(slots, normed, weights, cosine, sine, b_q)


def attend_kernel(meta, q, tail, *refs):
    kvs, (out, keys, values, turned, top, total, mixed, sems) = refs[:8], refs[8:]
    z, chunk, j = meta[0], meta[1], meta[2]
    factor = math.log2(math.e) / math.sqrt(HEAD)
    copies = []
    for index, ref in enumerate(kvs):
        place = (1 - j, j)[index] if index < 2 else index
        parts = [(ref.at[pl.ds(0, TOK)], keys.at[place])]
        for low in range(0, TOK, HEAD):
            parts.append(
                (ref.at[pl.ds(TOK + low, HEAD)], values.at[place, :, pl.ds(low, HEAD)])
            )
        for source, target in parts:
            copies.append(pltpu.make_async_copy(source, target, sems.at[len(copies)]))
    for copy in copies:
        copy.start()
    for head in range(5):
        span = slice(head * HEAD, (head + 1) * HEAD)
        turned[head] = q[:TOK, span].astype(jnp.float32).T.astype(jnp.bfloat16)
    top[...] = jnp.full_like(top, NEG)
    total[...] = jnp.zeros_like(total)
    mixed[...] = jnp.zeros_like(mixed)
    for copy in copies:
        copy.wait()

    def soften(scores, head, low):
        lanes = slice(low, low + scores.shape[1])
        before = top[head, :, lanes]
        now = jnp.maximum(before, jnp.max(scores, axis=0, keepdims=True))
        scale = jnp.exp2((before - now) * factor)
        expo = jnp.exp2(scores * factor - now * factor)
        top[head, :, lanes] = now
        total[head, :, lanes] = total[head, :, lanes] * scale + jnp.sum(
            expo, axis=0, keepdims=True
        )
        return expo.astype(jnp.bfloat16), scale

    def mix(softened, head, low, place):
        expo, scale = softened
        lanes = slice(low, low + expo.shape[1])
        mixed[head, :, lanes] = mixed[head, :, lanes] * scale + jnp.dot(
            values[place], expo, preferred_element_type=jnp.float32
        )

    units = [(head, low) for head in range(5) for low in range(0, TOK, WIDE)]

    def scores_of(head, low, place):
        query = turned[head, :, low : low + WIDE]
        return jnp.dot(keys[place], query, preferred_element_type=jnp.float32)

    def fold(place, masked):
        ahead = scores_of(*units[0], place)
        softened = None
        for index, (head, low) in enumerate(units):
            scores = ahead
            if index + 1 < len(units):
                ahead = scores_of(*units[index + 1], place)
            if masked:
                key = lax.broadcasted_iota(jnp.int32, scores.shape, 0)
                row = low + lax.broadcasted_iota(jnp.int32, scores.shape, 1)
                scores = jnp.where(key <= row, scores, NEG)
            now = soften(scores, head, low)
            if index > 0:
                mix(softened, *units[index - 1], place)
            softened = now
        mix(softened, *units[-1], place)

    def visit(place, _):
        fold(place, False)
        return 0

    fold(1 - chunk, True)
    lax.fori_loop(2 - chunk, 2 * z + 2, visit, 0)
    for head in range(5):
        span = slice(head * HEAD, (head + 1) * HEAD)
        out[:TOK, span] = (mixed[head] / total[head]).T.astype(jnp.bfloat16)

    size = ROWS - TOK
    blank = jnp.zeros((HEAD - 5 * size, HEAD), jnp.float32)
    query = [
        q[TOK:, head * HEAD : (head + 1) * HEAD].astype(jnp.float32) for head in range(5)
    ]
    query = jnp.concatenate(query + [blank], axis=0)
    own_key, own_value = [
        jnp.concatenate([tail[n].astype(jnp.float32)] * 5 + [blank], axis=0)
        for n in range(2)
    ]
    lanes = slice(0, HEAD)
    own = jnp.sum((query * own_key).T, axis=0, keepdims=True)
    top[0, :, lanes] = own
    total[0, :, lanes] = jnp.ones_like(own)
    mixed[0, :, lanes] = own_value.T
    query = query.T.astype(jnp.bfloat16)

    def visit_all(place, _):
        scores = jnp.dot(keys[place], query, preferred_element_type=jnp.float32)
        mix(soften(scores, 0, 0), 0, 0, place)
        return 0

    lax.fori_loop(0, 2 * SIZE, visit_all, 0)
    done = (mixed[0, :, lanes] / total[0, :, lanes]).T.astype(jnp.bfloat16)
    for head in range(5):
        out[TOK:, head * HEAD : (head + 1) * HEAD] = done[head * size : (head + 1) * size]


def attend(meta, query, tail, kvs):
    return pl.pallas_call(
        attend_kernel,
        out_shape=jax.ShapeDtypeStruct((ROWS, 5 * HEAD), jnp.bfloat16),
        in_specs=[SMEM_SPEC] + [VMEM_SPEC] * 2 + [ANY_SPEC] * 8,
        out_specs=VMEM_SPEC,
        scratch_shapes=[
            pltpu.VMEM((2 * SIZE, TOK, HEAD), jnp.bfloat16),
            pltpu.VMEM((2 * SIZE, HEAD, TOK), jnp.bfloat16),
            pltpu.VMEM((5, HEAD, TOK), jnp.bfloat16),
            pltpu.VMEM((5, 1, TOK), jnp.float32),
            pltpu.VMEM((5, 1, TOK), jnp.float32),
            pltpu.VMEM((5, HEAD, TOK), jnp.float32),
            pltpu.SemaphoreType.DMA((40,)),
        ],
        compiler_params=pltpu.CompilerParams(vmem_limit_bytes=VMEM),
        cost_estimate=pl.CostEstimate(
            flops=0, bytes_accessed=60 * 2**20, transcendentals=0
        ),
        name="attend",
    )(meta, query, tail, *kvs)


def select_kernel(place, arrived, out):
    spread = place[...] == lax.broadcasted_iota(jnp.int32, (ROWS, arrived.shape[0]), 1)
    out[...] = jnp.dot(
        spread.astype(jnp.bfloat16), arrived[...], preferred_element_type=jnp.float32
    ).astype(jnp.bfloat16)


def nought(array, limit):
    held = lax.optimization_barrier(array)[(0,) * array.ndim]
    return (held > limit).astype(jnp.int32)


def counts_before(flags):
    upto = jnp.arange(TOK)[:, None] <= jnp.arange(TOK)[None, :]
    return jnp.dot(
        flags.astype(jnp.bfloat16), upto.astype(jnp.bfloat16), preferred_element_type=jnp.float32
    ).astype(jnp.int32)


def local(
    prompt_ids,
    first_ids,
    table,
    norm_gain,
    slot_map,
    w_query,
    key_weight,
    value_weight,
    b_query,
    b_key,
    value_bias,
):
    ctx = lax.axis_index("ctx")
    tp = lax.axis_index("tp")
    y = lax.axis_index("grp")
    z, j = ctx // 2, ctx % 2
    x, core = (tp // 2) * 2 + j, tp % 2
    vocab_dev, features = table.shape
    samples = first_ids.shape[0]

    def columns(head):
        pick = lambda w, n: lax.dynamic_slice_in_dim(w, head * n, n, 2)
        return jnp.concatenate(
            [pick(w_query, 5 * HEAD), pick(key_weight, HEAD), pick(value_weight, HEAD)], axis=2
        )

    mine = jnp.concatenate([prompt_ids, first_ids])[None]
    both = jnp.concatenate([mine, move(mine, side=1)], axis=0)
    ids = jnp.concatenate([both, move(both, dz=-1), move(both, dz=2), move(both, dz=1)], axis=0)

    own = columns(j)
    give = columns(1 - j)
    first = y % 2
    near0 = move(lax.dynamic_index_in_dim(give, first, 0, keepdims=False), pair=1)

    wanted = ids - ctx * vocab_dev
    inside = (wanted >= 0) & (wanted < vocab_dev)
    rank = jnp.where(inside[:, :TOK], counts_before(inside[:, :TOK]) - 1, -1)
    at_slot = rank[:, None, :] == jnp.arange(CAP, dtype=jnp.int32)[None, :, None]
    chosen = jnp.sum(jnp.where(at_slot, wanted[:, None, :TOK], 0), axis=-1)
    chosen = jnp.concatenate(
        [
            chosen,
            jnp.where(inside[:, TOK:], wanted[:, TOK:], 0),
            jnp.zeros((8, MSG - CAP - samples), jnp.int32),
        ],
        axis=1,
    )
    chunks = jnp.arange(2 * SIZE, dtype=jnp.int32)
    lies = ((chunks // 2 - z) % SIZE) * 2 + (chunks + j) % 2
    chosen = jnp.sum(jnp.where((lies[:, None] == chunks)[:, :, None], chosen[None], 0), axis=1)
    wait_ids = nought(chosen, 1 << 30)
    part = jnp.where(
        j + wait_ids == y // 2, lax.dynamic_index_in_dim(own, first, 0, keepdims=False), near0
    )
    same_j = [[(2 * n + k) * SIZE + m for n in range(SIZE) for m in range(SIZE)] for k in (0, 1)]
    far_kv, far_q = [
        lax.all_gather(
            part[:, low:high], ("ctx", "grp"), axis_index_groups=same_j, axis=0, tiled=False
        )
        for low, high in ((5 * HEAD, 7 * HEAD), (0, 5 * HEAD))
    ]
    chosen = chosen + nought(part, 1000)
    message = table.at[chosen.reshape(-1)].get(mode="promise_in_bounds")
    arrived = lax.all_to_all(message, "ctx", 0, 0, tiled=True)

    wait_message = nought(message, 1000)
    owner = (mine[0] + wait_message) // vocab_dev
    held_by = owner[None, :TOK] == chunks[:, None]
    place = jnp.sum(jnp.where(held_by, counts_before(held_by) - 1, 0), axis=0)
    place = jnp.concatenate([place, CAP + jnp.arange(samples, dtype=jnp.int32)]) + owner * MSG
    place = jnp.concatenate([place, jnp.full((ROWS - TOK - samples,), -1, jnp.int32)])
    positions = jnp.arange(ROWS, dtype=jnp.int32) + wait_message
    tables = [
        rope_tables(jnp.where(positions < TOK, (2 * z + n) * TOK + positions, SIZE * 2 * TOK))
        for n in (j, 1 - j)
    ]
    meta = jnp.stack([x, z, y, j, core]).astype(jnp.int32)
    meta_own = jnp.stack([z, j, j]).astype(jnp.int32)
    meta_other = jnp.stack([z, 1 - j, j]).astype(jnp.int32)
    take = lambda vector, n: lax.dynamic_slice_in_dim(vector, j * n, n, 0)[None]
    gain, b_q, b_k, b_v = (
        norm_gain[None], take(b_query, 5 * HEAD), take(b_key, HEAD), take(value_bias, HEAD)
    )
    place, tables, meta, meta_own, meta_other, gain, b_q, b_k, b_v = lax.optimization_barrier(
        (place[:, None], tables, meta, meta_own, meta_other, gain, b_q, b_k, b_v)
    )
    embedded = pl.pallas_call(
        select_kernel,
        out_shape=jax.ShapeDtypeStruct((ROWS, features), jnp.bfloat16),
        compiler_params=pltpu.CompilerParams(vmem_limit_bytes=VMEM),
        cost_estimate=pl.CostEstimate(flops=0, bytes_accessed=14 * 2**20, transcendentals=0),
        name="select",
    )(place, arrived)

    left, right = move(embedded, dx=1), move(embedded, dx=-1)
    across = move(left[:CUT], dx=1), move(right[CUT:], dx=-1)

    def pieces(piece, dx, start=0):
        yield piece, (dx, False, start, piece.shape[0])
        yield move(piece, core=1), (dx, True, start, piece.shape[0])

    pieces_other = [*pieces(left, 3), *pieces(right, 1)]

    kvs, queries, tails = {}, {}, {}
    for name, (cosine, sine) in (("other", tables[1]), ("own", tables[0])):
        parts = pieces_other if name == "other" else pieces_own
        kv, tails[name], normed = project_kv(
            meta, slot_map, parts, far_kv, gain, cosine, sine, b_k, b_v
        )
        if name == "other":
            kv, *across = lax.optimization_barrier((kv, *across))
            pieces_own = [*pieces(embedded, 0), *pieces(across[0], 2), *pieces(across[1], 2, CUT)]
        kvs[name] = [kv] + [move(kv, dz=dz) for dz in (1, 2, 3)]
        queries[name] = project_q(slot_map, normed, far_q, cosine, sine, b_q)
    queries = lax.optimization_barrier(queries)
    every = [kv for pair in zip(kvs["own"], kvs["other"]) for kv in pair]
    theirs = move(attend(meta_other, queries["other"], tails["other"], every), pair=1)
    ours = attend(meta_own, queries["own"], tails["own"], every)
    heads = jnp.where(
        j == 0,
        jnp.concatenate([ours, theirs], axis=1),
        jnp.concatenate([theirs, ours], axis=1),
    )
    return heads[:TOK], heads[TOK : TOK + samples]


def solution(mesh):
    placed = (
        P(("grp", "ctx")),
        P(("grp", "ctx")),
        P("ctx", "tp"),
        P(),
        P(),
        P("ctx", None, "tp"),
        P("ctx", None, "tp"),
        P("ctx", None, "tp"),
        P("tp"),
        P("tp"),
        P("tp"),
    )
    return jax.shard_map(
        local,
        mesh=mesh,
        in_specs=placed,
        out_specs=(P(("grp", "ctx"), "tp"), P(("grp", "ctx"), "tp")),
        check_vma=False,
    )
```

```python
import functools
import math

import jax
import jax.numpy as jnp
from jax import lax
from jax.experimental import pallas as pl
from jax.experimental.pallas import tpu as pltpu
from jax.sharding import PartitionSpec as P

HEAD = 128
EPS = 1e-06
THETA = 1000000.0
NEG = -1e30
AXES = ("ctx", "tp", "grp")
CAP = 128
MSG = 136
ROWS = 528
TOK = 512
SIZE = 4
VMEM = 56 * 1024 * 1024
DEEP = 1280
CUT = 256
WIDE = 256
WIDE = 256
FAR_Z = (3, 1, 2)


def device_number(x, y, z, core):
    return ((z * 2 + x % 2) * 4 + (x // 2) * 2 + core) * 4 + y


def move(array, dx=0, dy=0, dz=0, pair=0, core=0, side=0):
    pairs = []
    for x in range(SIZE):
        for y in range(SIZE):
            for z in range(SIZE):
                for c in range(2):
                    along = (x + dx + side * (2 * (x % 2) - 1)) % SIZE
                    there = along ^ pair, (y + dy) % SIZE, (z + dz) % SIZE, c ^ core
                    pairs.append((device_number(x, y, z, c), device_number(*there)))
    return lax.ppermute(array, AXES, pairs)


def rope_tables(positions):
    half = HEAD // 2
    frequency = jnp.power(THETA, -jnp.arange(half, dtype=jnp.float32) * 2.0 / HEAD)
    angles = positions.astype(jnp.float32)[:, None] * frequency[None, :]
    cosine, sine = jnp.cos(angles), jnp.sin(angles)
    return jnp.concatenate([cosine, cosine], 1), jnp.concatenate([-sine, sine], 1)


def rotate(value, cosine, sine):
    return value * cosine + pltpu.roll(value, HEAD // 2, 1) * sine


def weight_copies(slots, weights, held, sems, low):
    span = pl.ds(low, held.shape[2])
    for bucket in range(16):
        slot = slots[bucket]
        source = weights.at[bucket, :, span]
        pltpu.make_async_copy(source, held.at[slot], sems.at[slot]).start()

    def wait(quarter):
        for slot in range(4 * quarter, 4 * quarter + 4):
            source = weights.at[0, :, span]
            pltpu.make_async_copy(source, held.at[slot], sems.at[slot]).wait()

    return wait


def multiply(k, rows, held, acc):
    product = jnp.dot(
        rows[:, k * DEEP : (k + 1) * DEEP],
        held[4 * k : 4 * k + 4].reshape(DEEP, held.shape[2]),
        preferred_element_type=jnp.float32,
    )
    acc[...] = product if k == 0 else acc[...] + product


def finish_q(acc, b_query, cosine, sine, q_out):
    for head in range(5):
        span = slice(head * HEAD, (head + 1) * HEAD)
        turned = rotate(acc[:, span] + b_query[:, span], cosine[...], sine[...])
        q_out[:, span] = turned.astype(jnp.bfloat16)


def kv_kernel(piece_at, fused, meta, slots, *refs):
    n = len(piece_at)
    weights, gain, cosine, sine, b_query, b_key, b_value = refs[n : n + 7]
    kv_out, tail_out, last_out, rows, held, acc, row_sems, held_sems, out_sem = refs[n + 7 :]
    x, core = meta[0], meta[4]
    low = 5 * HEAD if fused else 0
    copies = []
    for ref, (dx, other, start, count) in zip(refs, piece_at):
        there = lax.rem(x + dx, SIZE)
        feature = 2 * (there // 2) + (1 - core if other else core)
        width = ref.shape[1]
        target = rows.at[pl.ds(start, count), pl.ds(pl.multiple_of(feature * width, 128), width)]
        copies.append(pltpu.make_async_copy(ref, target, row_sems.at[len(copies)]))
    for copy in copies:
        copy.start()
    wait = weight_copies(slots, weights, held, held_sems, 5 * HEAD - low)
    for copy in copies:
        copy.wait()
    step = 48
    lanes = [slice(start, start + HEAD) for start in range(0, rows.shape[1], HEAD)]

    def normalize(index, _):
        span = pl.ds(pl.multiple_of(index * step, 16), step)
        squares = jnp.zeros((step, HEAD), jnp.float32)
        for lane in lanes:
            values = rows[span, lane].astype(jnp.float32)
            squares = squares + values * values
        mean = jnp.sum(squares, axis=-1, keepdims=True) / rows.shape[1]
        factor = lax.rsqrt(mean + EPS)
        for lane in lanes:
            values = rows[span, lane].astype(jnp.float32)
            rows[span, lane] = (values * factor * gain[:, lane]).astype(jnp.bfloat16)
        return 0

    lax.fori_loop(0, ROWS // step, normalize, 0)
    if not fused:
        out = pltpu.make_async_copy(rows, last_out, out_sem)
        out.start()
    for k in range(4):
        wait(k)
        multiply(k, rows, held, acc)
    key = rotate(acc[:, low : low + HEAD] + b_key[...], cosine[...], sine[...])
    value = acc[:, low + HEAD :] + b_value[...]
    kv_out[:TOK] = key[:TOK].astype(jnp.bfloat16)
    tail_out[0] = key[TOK:].astype(jnp.bfloat16)
    tail_out[1] = value[TOK:].astype(jnp.bfloat16)
    for start in range(0, TOK, HEAD):
        kv_out[TOK + start : TOK + start + HEAD] = (
            value[start : start + HEAD].T.astype(jnp.bfloat16)
        )
    if fused:
        finish_q(acc, b_query, cosine, sine, last_out)
    else:
        out.wait()


def q_kernel(
    slots, normed, weights, cosine, sine, b_query, q_out, rows, held, acc, row_sems, held_sems
):
    copies = []
    for k in range(4):
        span = pl.ds(k * DEEP, DEEP)
        copies.append(pltpu.make_async_copy(normed.at[:, span], rows.at[:, span], row_sems.at[k]))
    wait = weight_copies(slots, weights, held, held_sems, 0)
    for copy in copies:
        copy.start()
    for k in range(4):
        wait(k)
        copies[k].wait()
        multiply(k, rows, held, acc)
    finish_q(acc, b_query, cosine, sine, q_out)


SMEM_SPEC = pl.BlockSpec(memory_space=pltpu.SMEM)
VMEM_SPEC = pl.BlockSpec(memory_space=pltpu.VMEM)
ANY_SPEC = pl.BlockSpec(memory_space=pl.ANY)


def project_kv(fused, meta, slots, pieces, weights, gain, cosine, sine, b_q, b_k, b_v):
    width = 4 * DEEP
    columns = 7 * HEAD if fused else 2 * HEAD
    refs, piece_at = zip(*pieces)
    return pl.pallas_call(
        functools.partial(kv_kernel, piece_at, fused),
        out_shape=(
            jax.ShapeDtypeStruct((2 * TOK, HEAD), jnp.bfloat16),
            jax.ShapeDtypeStruct((2, ROWS - TOK, HEAD), jnp.bfloat16),
            jax.ShapeDtypeStruct((ROWS, 5 * HEAD if fused else width), jnp.bfloat16),
        ),
        in_specs=[SMEM_SPEC] * 2 + [ANY_SPEC] * (len(refs) + 1) + [VMEM_SPEC] * 6,
        out_specs=(VMEM_SPEC, VMEM_SPEC, VMEM_SPEC if fused else ANY_SPEC),
        scratch_shapes=[
            pltpu.VMEM((ROWS, width), jnp.bfloat16),
            pltpu.VMEM((16, 320, columns), jnp.bfloat16),
            pltpu.VMEM((ROWS, columns), jnp.float32),
            pltpu.SemaphoreType.DMA((len(refs),)),
            pltpu.SemaphoreType.DMA((16,)),
            pltpu.SemaphoreType.DMA,
        ],
        compiler_params=pltpu.CompilerParams(vmem_limit_bytes=VMEM),
        cost_estimate=pl.CostEstimate(
            flops=2 * ROWS * width * columns, bytes_accessed=30 * 2**20, transcendentals=0
        ),
        name="norm_qkv" if fused else "norm_kv",
    )(meta, slots, *refs, weights, gain, cosine, sine, b_q, b_k, b_v)


def project_q(slots, normed, weights, cosine, sine, b_q):
    width = 4 * DEEP
    return pl.pallas_call(
        q_kernel,
        out_shape=jax.ShapeDtypeStruct((ROWS, 5 * HEAD), jnp.bfloat16),
        in_specs=[SMEM_SPEC] + [ANY_SPEC] * 2 + [VMEM_SPEC] * 3,
        out_specs=VMEM_SPEC,
        scratch_shapes=[
            pltpu.VMEM((ROWS, width), jnp.bfloat16),
            pltpu.VMEM((16, 320, 5 * HEAD), jnp.bfloat16),
            pltpu.VMEM((ROWS, 5 * HEAD), jnp.float32),
            pltpu.SemaphoreType.DMA((4,)),
            pltpu.SemaphoreType.DMA((16,)),
        ],
        compiler_params=pltpu.CompilerParams(vmem_limit_bytes=VMEM),
        cost_estimate=pl.CostEstimate(
            flops=2 * ROWS * width * 5 * HEAD, bytes_accessed=24 * 2**20, transcendentals=0
        ),
        name="query",
    )(slots, normed, weights, cosine, sine, b_q)


def attend_kernel(meta, q, tail, *refs):
    kvs, (out, keys, values, turned, top, total, mixed, sems) = refs[:8], refs[8:]
    z, chunk, j = meta[0], meta[1], meta[2]
    factor = math.log2(math.e) / math.sqrt(HEAD)
    copies = []
    for index, ref in enumerate(kvs):
        place = (1 - j, j)[index] if index < 2 else index
        parts = [(ref.at[pl.ds(0, TOK)], keys.at[pl.ds(place * TOK, TOK)])]
        for low in range(0, TOK, HEAD):
            parts.append(
                (ref.at[pl.ds(TOK + low, HEAD)], values.at[:, pl.ds(place * TOK + low, HEAD)])
            )
        for source, target in parts:
            copies.append(pltpu.make_async_copy(source, target, sems.at[len(copies)]))
    for copy in copies:
        copy.start()
    for head in range(5):
        span = slice(head * HEAD, (head + 1) * HEAD)
        turned[head] = q[:TOK, span].astype(jnp.float32).T.astype(jnp.bfloat16)
    top[...] = jnp.full_like(top, NEG)
    total[...] = jnp.zeros_like(total)
    mixed[...] = jnp.zeros_like(mixed)
    for copy in copies:
        copy.wait()

    def soften(scores, head, low):
        lanes = slice(low, low + scores.shape[1])
        before = top[head, :, lanes]
        now = jnp.maximum(before, jnp.max(scores, axis=0, keepdims=True))
        scale = jnp.exp2((before - now) * factor)
        expo = jnp.exp2(scores * factor - now * factor)
        top[head, :, lanes] = now
        total[head, :, lanes] = total[head, :, lanes] * scale + jnp.sum(
            expo, axis=0, keepdims=True
        )
        return expo.astype(jnp.bfloat16), scale

    def mix(softened, head, low, there):
        expo, scale = softened
        lanes = slice(low, low + expo.shape[1])
        mixed[head, :, lanes] = mixed[head, :, lanes] * scale + jnp.dot(
            values[:, there], expo, preferred_element_type=jnp.float32
        )

    units = [(head, low) for head in range(5) for low in range(0, TOK, WIDE)]

    def scores_of(head, low, there):
        query = turned[head, :, low : low + WIDE]
        return jnp.dot(keys[there, :], query, preferred_element_type=jnp.float32)

    def fold(start, size, masked=False):
        there = pl.ds(pl.multiple_of(start, TOK), size)
        ahead = scores_of(*units[0], there)
        softened = None
        for index, (head, low) in enumerate(units):
            scores = ahead
            if index + 1 < len(units):
                ahead = scores_of(*units[index + 1], there)
            if masked:
                key = lax.broadcasted_iota(jnp.int32, scores.shape, 0)
                row = low + lax.broadcasted_iota(jnp.int32, scores.shape, 1)
                scores = jnp.where(key <= row, scores, NEG)
            now = soften(scores, head, low)
            if index > 0:
                mix(softened, *units[index - 1], there)
            softened = now
        mix(softened, *units[-1], there)

    def visit(away, _):
        fold(away * 2 * TOK, 2 * TOK)
        return 0

    fold((1 - chunk) * TOK, TOK, True)

    @pl.when(chunk == 1)
    def _():
        fold(TOK, TOK)

    lax.fori_loop(1, z + 1, visit, 0)
    for head in range(5):
        span = slice(head * HEAD, (head + 1) * HEAD)
        out[:TOK, span] = (mixed[head] / total[head]).T.astype(jnp.bfloat16)

    size = ROWS - TOK
    blank = jnp.zeros((HEAD - 5 * size, HEAD), jnp.float32)
    query = [
        q[TOK:, head * HEAD : (head + 1) * HEAD].astype(jnp.float32) for head in range(5)
    ]
    query = jnp.concatenate(query + [blank], axis=0)
    own_key, own_value = [
        jnp.concatenate([tail[n].astype(jnp.float32)] * 5 + [blank], axis=0)
        for n in range(2)
    ]
    lanes = slice(0, HEAD)
    own = jnp.sum((query * own_key).T, axis=0, keepdims=True)
    top[0, :, lanes] = own
    total[0, :, lanes] = jnp.ones_like(own)
    mixed[0, :, lanes] = own_value.T
    query = query.T.astype(jnp.bfloat16)

    def visit_all(away, _):
        there = pl.ds(pl.multiple_of(away * 2 * TOK, TOK), 2 * TOK)
        scores = jnp.dot(keys[there, :], query, preferred_element_type=jnp.float32)
        mix(soften(scores, 0, 0), 0, 0, there)
        return 0

    lax.fori_loop(0, SIZE, visit_all, 0)
    done = (mixed[0, :, lanes] / total[0, :, lanes]).T.astype(jnp.bfloat16)
    for head in range(5):
        out[TOK:, head * HEAD : (head + 1) * HEAD] = done[head * size : (head + 1) * size]


def attend(meta, query, tail, kvs):
    return pl.pallas_call(
        attend_kernel,
        out_shape=jax.ShapeDtypeStruct((ROWS, 5 * HEAD), jnp.bfloat16),
        in_specs=[SMEM_SPEC] + [VMEM_SPEC] * 2 + [ANY_SPEC] * 8,
        out_specs=VMEM_SPEC,
        scratch_shapes=[
            pltpu.VMEM((2 * SIZE * TOK, HEAD), jnp.bfloat16),
            pltpu.VMEM((HEAD, 2 * SIZE * TOK), jnp.bfloat16),
            pltpu.VMEM((5, HEAD, TOK), jnp.bfloat16),
            pltpu.VMEM((5, 1, TOK), jnp.float32),
            pltpu.VMEM((5, 1, TOK), jnp.float32),
            pltpu.VMEM((5, HEAD, TOK), jnp.float32),
            pltpu.SemaphoreType.DMA((40,)),
        ],
        compiler_params=pltpu.CompilerParams(vmem_limit_bytes=VMEM),
        cost_estimate=pl.CostEstimate(
            flops=0, bytes_accessed=60 * 2**20, transcendentals=0
        ),
        name="attend",
    )(meta, query, tail, *kvs)


def select_kernel(place, arrived, out):
    spread = place[...] == lax.broadcasted_iota(jnp.int32, (ROWS, arrived.shape[0]), 1)
    out[...] = jnp.dot(
        spread.astype(jnp.bfloat16), arrived[...], preferred_element_type=jnp.float32
    ).astype(jnp.bfloat16)


def nought(array, limit):
    held = lax.optimization_barrier(array)[(0,) * array.ndim]
    return (held > limit).astype(jnp.int32)


def counts_before(flags):
    upto = jnp.arange(TOK)[:, None] <= jnp.arange(TOK)[None, :]
    return jnp.dot(
        flags.astype(jnp.bfloat16), upto.astype(jnp.bfloat16), preferred_element_type=jnp.float32
    ).astype(jnp.int32)


def local(
    prompt_ids,
    first_ids,
    table,
    norm_gain,
    slot_map,
    w_query,
    key_weight,
    value_weight,
    b_query,
    b_key,
    value_bias,
):
    ctx = lax.axis_index("ctx")
    tp = lax.axis_index("tp")
    y = lax.axis_index("grp")
    z, j = ctx // 2, ctx % 2
    x, core = (tp // 2) * 2 + j, tp % 2
    vocab_dev, features = table.shape
    samples = first_ids.shape[0]

    def columns(head):
        pick = lambda w, n: lax.dynamic_slice_in_dim(w, head * n, n, 2)
        return jnp.concatenate(
            [pick(w_query, 5 * HEAD), pick(key_weight, HEAD), pick(value_weight, HEAD)], axis=2
        )

    mine = jnp.concatenate([prompt_ids, first_ids])[None]
    both = jnp.concatenate([mine, move(mine, side=1)], axis=0)
    ids = jnp.concatenate([both, move(both, dz=-1), move(both, dz=2), move(both, dz=1)], axis=0)

    own = columns(j)
    give = columns(1 - j)
    first = y % 2
    near0 = move(lax.dynamic_index_in_dim(give, first, 0, keepdims=False), pair=1)

    wanted = ids - ctx * vocab_dev
    inside = (wanted >= 0) & (wanted < vocab_dev)
    rank = jnp.where(inside[:, :TOK], counts_before(inside[:, :TOK]) - 1, -1)
    at_slot = rank[:, None, :] == jnp.arange(CAP, dtype=jnp.int32)[None, :, None]
    chosen = jnp.sum(jnp.where(at_slot, wanted[:, None, :TOK], 0), axis=-1)
    chosen = jnp.concatenate(
        [
            chosen,
            jnp.where(inside[:, TOK:], wanted[:, TOK:], 0),
            jnp.zeros((8, MSG - CAP - samples), jnp.int32),
        ],
        axis=1,
    )
    chunks = jnp.arange(2 * SIZE, dtype=jnp.int32)
    lies = ((chunks // 2 - z) % SIZE) * 2 + (chunks + j) % 2
    chosen = jnp.sum(jnp.where((lies[:, None] == chunks)[:, :, None], chosen[None], 0), axis=1)
    wait_ids = nought(chosen, 1 << 30)
    part = jnp.where(
        j + wait_ids == y // 2, lax.dynamic_index_in_dim(own, first, 0, keepdims=False), near0
    )
    same_j = [[(2 * n + k) * SIZE + m for n in range(SIZE) for m in range(SIZE)] for k in (0, 1)]
    weights = lax.all_gather(
        part, ("ctx", "grp"), axis_index_groups=same_j, axis=0, tiled=False
    )
    chosen = chosen + nought(part, 1000)
    message = table.at[chosen.reshape(-1)].get(mode="promise_in_bounds")
    arrived = lax.all_to_all(message, "ctx", 0, 0, tiled=True)

    wait_message = nought(message, 1000)
    owner = (mine[0] + wait_message) // vocab_dev
    held_by = owner[None, :TOK] == chunks[:, None]
    place = jnp.sum(jnp.where(held_by, counts_before(held_by) - 1, 0), axis=0)
    place = jnp.concatenate([place, CAP + jnp.arange(samples, dtype=jnp.int32)]) + owner * MSG
    place = jnp.concatenate([place, jnp.full((ROWS - TOK - samples,), -1, jnp.int32)])
    positions = jnp.arange(ROWS, dtype=jnp.int32) + wait_message
    tables = [
        rope_tables(jnp.where(positions < TOK, (2 * z + n) * TOK + positions, SIZE * 2 * TOK))
        for n in (j, 1 - j)
    ]
    meta = jnp.stack([x, z, y, j, core]).astype(jnp.int32)
    meta_own = jnp.stack([z, j, j]).astype(jnp.int32)
    meta_other = jnp.stack([z, 1 - j, j]).astype(jnp.int32)
    take = lambda vector, n: lax.dynamic_slice_in_dim(vector, j * n, n, 0)[None]
    gain, b_q, b_k, b_v = (
        norm_gain[None], take(b_query, 5 * HEAD), take(b_key, HEAD), take(value_bias, HEAD)
    )
    place, tables, meta, meta_own, meta_other, gain, b_q, b_k, b_v = lax.optimization_barrier(
        (place[:, None], tables, meta, meta_own, meta_other, gain, b_q, b_k, b_v)
    )
    embedded = pl.pallas_call(
        select_kernel,
        out_shape=jax.ShapeDtypeStruct((ROWS, features), jnp.bfloat16),
        compiler_params=pltpu.CompilerParams(vmem_limit_bytes=VMEM),
        cost_estimate=pl.CostEstimate(flops=0, bytes_accessed=14 * 2**20, transcendentals=0),
        name="select",
    )(place, arrived)

    left, right = move(embedded, dx=1), move(embedded, dx=-1)
    across = move(left[:CUT], dx=1), move(right[CUT:], dx=-1)

    def pieces(piece, dx, start=0):
        yield piece, (dx, False, start, piece.shape[0])
        yield move(piece, core=1), (dx, True, start, piece.shape[0])

    pieces_other = [*pieces(left, 3), *pieces(right, 1)]

    kvs, queries, tails = {}, {}, {}
    kv, tails["other"], queries["other"] = project_kv(
        True, meta, slot_map, pieces_other, weights, gain, *tables[1], b_q, b_k, b_v
    )
    kv, *across = lax.optimization_barrier((kv, *across))
    kvs["other"] = [kv] + [move(kv, dz=dz) for dz in (1, 2, 3)]
    pieces_own = [*pieces(embedded, 0), *pieces(across[0], 2), *pieces(across[1], 2, CUT)]
    kv, tails["own"], normed = project_kv(
        False, meta, slot_map, pieces_own, weights, gain, *tables[0], b_q, b_k, b_v
    )
    kvs["own"] = [kv] + [move(kv, dz=dz) for dz in (1, 2, 3)]
    queries["own"] = project_q(slot_map, normed, weights, *tables[0], b_q)
    queries = lax.optimization_barrier(queries)
    every = [kv for pair in zip(kvs["own"], kvs["other"]) for kv in pair]
    theirs = move(attend(meta_other, queries["other"], tails["other"], every), pair=1)
    ours = attend(meta_own, queries["own"], tails["own"], every)
    heads = jnp.where(
        j == 0,
        jnp.concatenate([ours, theirs], axis=1),
        jnp.concatenate([theirs, ours], axis=1),
    )
    return heads[:TOK], heads[TOK : TOK + samples]


def solution(mesh):
    placed = (
        P(("grp", "ctx")),
        P(("grp", "ctx")),
        P("ctx", "tp"),
        P(),
        P(),
        P("ctx", None, "tp"),
        P("ctx", None, "tp"),
        P("ctx", None, "tp"),
        P("tp"),
        P("tp"),
        P("tp"),
    )
    return jax.shard_map(
        local,
        mesh=mesh,
        in_specs=placed,
        out_specs=(P(("grp", "ctx"), "tp"), P(("grp", "ctx"), "tp")),
        check_vma=False,
    )
```

```python
import functools
import math

import jax
import jax.numpy as jnp
from jax import lax
from jax.experimental import pallas as pl
from jax.experimental.pallas import tpu as pltpu
from jax.sharding import PartitionSpec as P

HEAD = 128
EPS = 1e-06
THETA = 1000000.0
NEG = -1e30
AXES = ("ctx", "tp", "grp")
CAP = 128
MSG = 136
ROWS = 528
TOK = 512
SIZE = 4
VMEM = 56 * 1024 * 1024
DEEP = 1280
CUT = 256
WIDE = 256
WIDE = 256
FAR_Z = (3, 1, 2)


def device_number(x, y, z, core):
    return ((z * 2 + x % 2) * 4 + (x // 2) * 2 + core) * 4 + y


def move(array, dx=0, dy=0, dz=0, pair=0, core=0, side=0):
    pairs = []
    for x in range(SIZE):
        for y in range(SIZE):
            for z in range(SIZE):
                for c in range(2):
                    along = (x + dx + side * (2 * (x % 2) - 1)) % SIZE
                    there = along ^ pair, (y + dy) % SIZE, (z + dz) % SIZE, c ^ core
                    pairs.append((device_number(x, y, z, c), device_number(*there)))
    return lax.ppermute(array, AXES, pairs)


def rope_tables(positions):
    half = HEAD // 2
    frequency = jnp.power(THETA, -jnp.arange(half, dtype=jnp.float32) * 2.0 / HEAD)
    angles = positions.astype(jnp.float32)[:, None] * frequency[None, :]
    cosine, sine = jnp.cos(angles), jnp.sin(angles)
    return jnp.concatenate([cosine, cosine], 1), jnp.concatenate([-sine, sine], 1)


def rotate(value, cosine, sine):
    return value * cosine + pltpu.roll(value, HEAD // 2, 1) * sine


def weight_copies(slots, weights, held, sems, low):
    span = pl.ds(low, held.shape[2])
    for bucket in range(16):
        slot = slots[bucket]
        source = weights.at[bucket, :, span]
        pltpu.make_async_copy(source, held.at[slot], sems.at[slot]).start()

    def wait(quarter):
        for slot in range(4 * quarter, 4 * quarter + 4):
            source = weights.at[0, :, span]
            pltpu.make_async_copy(source, held.at[slot], sems.at[slot]).wait()

    return wait


def multiply(k, rows, held, acc):
    product = jnp.dot(
        rows[:, k * DEEP : (k + 1) * DEEP],
        held[4 * k : 4 * k + 4].reshape(DEEP, held.shape[2]),
        preferred_element_type=jnp.float32,
    )
    acc[...] = product if k == 0 else acc[...] + product


def finish_q(acc, b_query, cosine, sine, q_out):
    for head in range(5):
        span = slice(head * HEAD, (head + 1) * HEAD)
        turned = rotate(acc[:, span] + b_query[:, span], cosine[...], sine[...])
        q_out[:, span] = turned.astype(jnp.bfloat16)


def kv_kernel(piece_at, fused, meta, slots, *refs):
    n = len(piece_at)
    weights, gain, cosine, sine, b_query, b_key, b_value = refs[n : n + 7]
    kv_out, tail_out, last_out, rows, held, acc, row_sems, held_sems, out_sem = refs[n + 7 :]
    x, core = meta[0], meta[4]
    low = 5 * HEAD if fused else 0
    copies = []
    for ref, (dx, other, start, count) in zip(refs, piece_at):
        there = lax.rem(x + dx, SIZE)
        feature = 2 * (there // 2) + (1 - core if other else core)
        width = ref.shape[1]
        target = rows.at[pl.ds(start, count), pl.ds(pl.multiple_of(feature * width, 128), width)]
        copies.append(pltpu.make_async_copy(ref, target, row_sems.at[len(copies)]))
    for copy in copies:
        copy.start()
    wait = weight_copies(slots, weights, held, held_sems, 5 * HEAD - low)
    for copy in copies:
        copy.wait()
    step = 48
    lanes = [slice(start, start + HEAD) for start in range(0, rows.shape[1], HEAD)]

    def normalize(index, _):
        span = pl.ds(pl.multiple_of(index * step, 16), step)
        squares = jnp.zeros((step, HEAD), jnp.float32)
        for lane in lanes:
            values = rows[span, lane].astype(jnp.float32)
            squares = squares + values * values
        mean = jnp.sum(squares, axis=-1, keepdims=True) / rows.shape[1]
        factor = lax.rsqrt(mean + EPS)
        for lane in lanes:
            values = rows[span, lane].astype(jnp.float32)
            rows[span, lane] = (values * factor * gain[:, lane]).astype(jnp.bfloat16)
        return 0

    lax.fori_loop(0, ROWS // step, normalize, 0)
    if not fused:
        out = pltpu.make_async_copy(rows, last_out, out_sem)
        out.start()
    for k in range(4):
        wait(k)
        multiply(k, rows, held, acc)
    key = rotate(acc[:, low : low + HEAD] + b_key[...], cosine[...], sine[...])
    value = acc[:, low + HEAD :] + b_value[...]
    kv_out[:TOK] = key[:TOK].astype(jnp.bfloat16)
    tail_out[0] = key[TOK:].astype(jnp.bfloat16)
    tail_out[1] = value[TOK:].astype(jnp.bfloat16)
    for start in range(0, TOK, HEAD):
        kv_out[TOK + start : TOK + start + HEAD] = (
            value[start : start + HEAD].T.astype(jnp.bfloat16)
        )
    if fused:
        finish_q(acc, b_query, cosine, sine, last_out)
    else:
        out.wait()


def q_kernel(
    slots, normed, weights, cosine, sine, b_query, q_out, rows, held, acc, row_sems, held_sems
):
    copies = []
    for k in range(4):
        span = pl.ds(k * DEEP, DEEP)
        copies.append(pltpu.make_async_copy(normed.at[:, span], rows.at[:, span], row_sems.at[k]))
    wait = weight_copies(slots, weights, held, held_sems, 0)
    for copy in copies:
        copy.start()
    for k in range(4):
        wait(k)
        copies[k].wait()
        multiply(k, rows, held, acc)
    finish_q(acc, b_query, cosine, sine, q_out)


SMEM_SPEC = pl.BlockSpec(memory_space=pltpu.SMEM)
VMEM_SPEC = pl.BlockSpec(memory_space=pltpu.VMEM)
ANY_SPEC = pl.BlockSpec(memory_space=pl.ANY)


def project_kv(fused, meta, slots, pieces, weights, gain, cosine, sine, b_q, b_k, b_v):
    width = 4 * DEEP
    columns = 7 * HEAD if fused else 2 * HEAD
    refs, piece_at = zip(*pieces)
    return pl.pallas_call(
        functools.partial(kv_kernel, piece_at, fused),
        out_shape=(
            jax.ShapeDtypeStruct((2 * TOK, HEAD), jnp.bfloat16),
            jax.ShapeDtypeStruct((2, ROWS - TOK, HEAD), jnp.bfloat16),
            jax.ShapeDtypeStruct((ROWS, 5 * HEAD if fused else width), jnp.bfloat16),
        ),
        in_specs=[SMEM_SPEC] * 2 + [ANY_SPEC] * (len(refs) + 1) + [VMEM_SPEC] * 6,
        out_specs=(VMEM_SPEC, VMEM_SPEC, VMEM_SPEC if fused else ANY_SPEC),
        scratch_shapes=[
            pltpu.VMEM((ROWS, width), jnp.bfloat16),
            pltpu.VMEM((16, 320, columns), jnp.bfloat16),
            pltpu.VMEM((ROWS, columns), jnp.float32),
            pltpu.SemaphoreType.DMA((len(refs),)),
            pltpu.SemaphoreType.DMA((16,)),
            pltpu.SemaphoreType.DMA,
        ],
        compiler_params=pltpu.CompilerParams(vmem_limit_bytes=VMEM),
        cost_estimate=pl.CostEstimate(
            flops=2 * ROWS * width * columns, bytes_accessed=30 * 2**20, transcendentals=0
        ),
        name="norm_qkv" if fused else "norm_kv",
    )(meta, slots, *refs, weights, gain, cosine, sine, b_q, b_k, b_v)


def project_q(slots, normed, weights, cosine, sine, b_q):
    width = 4 * DEEP
    return pl.pallas_call(
        q_kernel,
        out_shape=jax.ShapeDtypeStruct((ROWS, 5 * HEAD), jnp.bfloat16),
        in_specs=[SMEM_SPEC] + [ANY_SPEC] * 2 + [VMEM_SPEC] * 3,
        out_specs=VMEM_SPEC,
        scratch_shapes=[
            pltpu.VMEM((ROWS, width), jnp.bfloat16),
            pltpu.VMEM((16, 320, 5 * HEAD), jnp.bfloat16),
            pltpu.VMEM((ROWS, 5 * HEAD), jnp.float32),
            pltpu.SemaphoreType.DMA((4,)),
            pltpu.SemaphoreType.DMA((16,)),
        ],
        compiler_params=pltpu.CompilerParams(vmem_limit_bytes=VMEM),
        cost_estimate=pl.CostEstimate(
            flops=2 * ROWS * width * 5 * HEAD, bytes_accessed=24 * 2**20, transcendentals=0
        ),
        name="query",
    )(slots, normed, weights, cosine, sine, b_q)


def attend_kernel(meta, q, tail, *refs):
    kvs, (out, keys, values, turned, top, total, mixed, sems) = refs[:8], refs[8:]
    z, chunk, j = meta[0], meta[1], meta[2]
    factor = math.log2(math.e) / math.sqrt(HEAD)
    copies = []
    for index, ref in enumerate(kvs):
        place = (1 - j, j)[index] if index < 2 else index
        parts = [(ref.at[pl.ds(0, TOK)], keys.at[pl.ds(place * TOK, TOK)])]
        for low in range(0, TOK, HEAD):
            parts.append(
                (ref.at[pl.ds(TOK + low, HEAD)], values.at[:, pl.ds(place * TOK + low, HEAD)])
            )
        for source, target in parts:
            copies.append(pltpu.make_async_copy(source, target, sems.at[len(copies)]))
    for copy in copies:
        copy.start()
    for head in range(5):
        span = slice(head * HEAD, (head + 1) * HEAD)
        turned[head] = q[:TOK, span].astype(jnp.float32).T.astype(jnp.bfloat16)
    top[...] = jnp.full_like(top, NEG)
    total[...] = jnp.zeros_like(total)
    mixed[...] = jnp.zeros_like(mixed)
    for copy in copies[:10]:
        copy.wait()

    def soften(scores, head, low):
        lanes = slice(low, low + scores.shape[1])
        before = top[head, :, lanes]
        now = jnp.maximum(before, jnp.max(scores, axis=0, keepdims=True))
        scale = jnp.exp2((before - now) * factor)
        expo = jnp.exp2(scores * factor - now * factor)
        top[head, :, lanes] = now
        total[head, :, lanes] = total[head, :, lanes] * scale + jnp.sum(
            expo, axis=0, keepdims=True
        )
        return expo.astype(jnp.bfloat16), scale

    def mix(softened, head, low, there):
        expo, scale = softened
        lanes = slice(low, low + expo.shape[1])
        mixed[head, :, lanes] = mixed[head, :, lanes] * scale + jnp.dot(
            values[:, there], expo, preferred_element_type=jnp.float32
        )

    units = [(head, low) for head in range(5) for low in range(0, TOK, WIDE)]

    def scores_of(head, low, there):
        query = turned[head, :, low : low + WIDE]
        return jnp.dot(keys[there, :], query, preferred_element_type=jnp.float32)

    def fold(start, size, masked=False):
        def there(low):
            return pl.ds(pl.multiple_of(start, TOK), low + WIDE if masked else size)

        ahead = scores_of(*units[0], there(0))
        softened = None
        for index, (head, low) in enumerate(units):
            scores = ahead
            if index + 1 < len(units):
                ahead = scores_of(*units[index + 1], there(units[index + 1][1]))
            if masked:
                key = lax.broadcasted_iota(jnp.int32, scores.shape, 0)
                row = low + lax.broadcasted_iota(jnp.int32, scores.shape, 1)
                scores = jnp.where(key <= row, scores, NEG)
            now = soften(scores, head, low)
            if index > 0:
                mix(softened, *units[index - 1], there(units[index - 1][1]))
            softened = now
        mix(softened, *units[-1], there(units[-1][1]))

    fold((1 - chunk) * TOK, TOK, True)
    for copy in copies[10:]:
        copy.wait()

    @pl.when(chunk == 1)
    def _():
        fold(TOK, TOK)

    @pl.when(z >= 2)
    def _():
        fold(2 * TOK, 4 * TOK)

    @pl.when(lax.rem(z, 2) == 1)
    def _():
        fold(z * 2 * TOK, 2 * TOK)

    for head in range(5):
        span = slice(head * HEAD, (head + 1) * HEAD)
        out[:TOK, span] = (mixed[head] / total[head]).T.astype(jnp.bfloat16)

    size = ROWS - TOK
    blank = jnp.zeros((HEAD - 5 * size, HEAD), jnp.float32)
    query = [
        q[TOK:, head * HEAD : (head + 1) * HEAD].astype(jnp.float32) for head in range(5)
    ]
    query = jnp.concatenate(query + [blank], axis=0)
    own_key, own_value = [
        jnp.concatenate([tail[n].astype(jnp.float32)] * 5 + [blank], axis=0)
        for n in range(2)
    ]
    lanes = slice(0, HEAD)
    own = jnp.sum((query * own_key).T, axis=0, keepdims=True)
    top[0, :, lanes] = own
    total[0, :, lanes] = jnp.ones_like(own)
    mixed[0, :, lanes] = own_value.T
    query = query.T.astype(jnp.bfloat16)

    def visit_all(away, _):
        there = pl.ds(pl.multiple_of(away * 2 * TOK, TOK), 2 * TOK)
        scores = jnp.dot(keys[there, :], query, preferred_element_type=jnp.float32)
        mix(soften(scores, 0, 0), 0, 0, there)
        return 0

    lax.fori_loop(0, SIZE, visit_all, 0)
    done = (mixed[0, :, lanes] / total[0, :, lanes]).T.astype(jnp.bfloat16)
    for head in range(5):
        out[TOK:, head * HEAD : (head + 1) * HEAD] = done[head * size : (head + 1) * size]


def attend(meta, query, tail, kvs):
    return pl.pallas_call(
        attend_kernel,
        out_shape=jax.ShapeDtypeStruct((ROWS, 5 * HEAD), jnp.bfloat16),
        in_specs=[SMEM_SPEC] + [VMEM_SPEC] * 2 + [ANY_SPEC] * 8,
        out_specs=VMEM_SPEC,
        scratch_shapes=[
            pltpu.VMEM((2 * SIZE * TOK, HEAD), jnp.bfloat16),
            pltpu.VMEM((HEAD, 2 * SIZE * TOK), jnp.bfloat16),
            pltpu.VMEM((5, HEAD, TOK), jnp.bfloat16),
            pltpu.VMEM((5, 1, TOK), jnp.float32),
            pltpu.VMEM((5, 1, TOK), jnp.float32),
            pltpu.VMEM((5, HEAD, TOK), jnp.float32),
            pltpu.SemaphoreType.DMA((40,)),
        ],
        compiler_params=pltpu.CompilerParams(vmem_limit_bytes=VMEM),
        cost_estimate=pl.CostEstimate(
            flops=0, bytes_accessed=60 * 2**20, transcendentals=0
        ),
        name="attend",
    )(meta, query, tail, *kvs)


def select_kernel(place, arrived, out):
    spread = place[...] == lax.broadcasted_iota(jnp.int32, (ROWS, arrived.shape[0]), 1)
    out[...] = jnp.dot(
        spread.astype(jnp.bfloat16), arrived[...], preferred_element_type=jnp.float32
    ).astype(jnp.bfloat16)


def nought(array, limit):
    held = lax.optimization_barrier(array)[(0,) * array.ndim]
    return (held > limit).astype(jnp.int32)


def counts_before(flags):
    upto = jnp.arange(TOK)[:, None] <= jnp.arange(TOK)[None, :]
    return jnp.dot(
        flags.astype(jnp.bfloat16), upto.astype(jnp.bfloat16), preferred_element_type=jnp.float32
    ).astype(jnp.int32)


def local(
    prompt_ids,
    first_ids,
    table,
    norm_gain,
    slot_map,
    w_query,
    key_weight,
    value_weight,
    b_query,
    b_key,
    value_bias,
):
    ctx = lax.axis_index("ctx")
    tp = lax.axis_index("tp")
    y = lax.axis_index("grp")
    z, j = ctx // 2, ctx % 2
    x, core = (tp // 2) * 2 + j, tp % 2
    vocab_dev, features = table.shape
    samples = first_ids.shape[0]

    def columns(head):
        pick = lambda w, n: lax.dynamic_slice_in_dim(w, head * n, n, 2)
        return jnp.concatenate(
            [pick(w_query, 5 * HEAD), pick(key_weight, HEAD), pick(value_weight, HEAD)], axis=2
        )

    mine = jnp.concatenate([prompt_ids, first_ids])[None]
    both = jnp.concatenate([mine, move(mine, side=1)], axis=0)
    ids = jnp.concatenate([both, move(both, dz=-1), move(both, dz=2), move(both, dz=1)], axis=0)

    own = columns(j)
    give = columns(1 - j)
    first = y % 2
    near0 = move(lax.dynamic_index_in_dim(give, first, 0, keepdims=False), pair=1)

    wanted = ids - ctx * vocab_dev
    inside = (wanted >= 0) & (wanted < vocab_dev)
    rank = jnp.where(inside[:, :TOK], counts_before(inside[:, :TOK]) - 1, -1)
    at_slot = rank[:, None, :] == jnp.arange(CAP, dtype=jnp.int32)[None, :, None]
    chosen = jnp.sum(jnp.where(at_slot, wanted[:, None, :TOK], 0), axis=-1)
    chosen = jnp.concatenate(
        [
            chosen,
            jnp.where(inside[:, TOK:], wanted[:, TOK:], 0),
            jnp.zeros((8, MSG - CAP - samples), jnp.int32),
        ],
        axis=1,
    )
    chunks = jnp.arange(2 * SIZE, dtype=jnp.int32)
    lies = ((chunks // 2 - z) % SIZE) * 2 + (chunks + j) % 2
    chosen = jnp.sum(jnp.where((lies[:, None] == chunks)[:, :, None], chosen[None], 0), axis=1)
    wait_ids = nought(chosen, 1 << 30)
    part = jnp.where(
        j + wait_ids == y // 2, lax.dynamic_index_in_dim(own, first, 0, keepdims=False), near0
    )
    same_j = [[(2 * n + k) * SIZE + m for n in range(SIZE) for m in range(SIZE)] for k in (0, 1)]
    weights = lax.all_gather(
        part, ("ctx", "grp"), axis_index_groups=same_j, axis=0, tiled=False
    )
    chosen = chosen + nought(part, 1000)
    message = table.at[chosen.reshape(-1)].get(mode="promise_in_bounds")
    arrived = lax.all_to_all(message, "ctx", 0, 0, tiled=True)

    wait_message = nought(message, 1000)
    owner = (mine[0] + wait_message) // vocab_dev
    held_by = owner[None, :TOK] == chunks[:, None]
    place = jnp.sum(jnp.where(held_by, counts_before(held_by) - 1, 0), axis=0)
    place = jnp.concatenate([place, CAP + jnp.arange(samples, dtype=jnp.int32)]) + owner * MSG
    place = jnp.concatenate([place, jnp.full((ROWS - TOK - samples,), -1, jnp.int32)])
    positions = jnp.arange(ROWS, dtype=jnp.int32) + wait_message
    tables = [
        rope_tables(jnp.where(positions < TOK, (2 * z + n) * TOK + positions, SIZE * 2 * TOK))
        for n in (j, 1 - j)
    ]
    meta = jnp.stack([x, z, y, j, core]).astype(jnp.int32)
    meta_own = jnp.stack([z, j, j]).astype(jnp.int32)
    meta_other = jnp.stack([z, 1 - j, j]).astype(jnp.int32)
    take = lambda vector, n: lax.dynamic_slice_in_dim(vector, j * n, n, 0)[None]
    gain, b_q, b_k, b_v = (
        norm_gain[None], take(b_query, 5 * HEAD), take(b_key, HEAD), take(value_bias, HEAD)
    )
    place, tables, meta, meta_own, meta_other, gain, b_q, b_k, b_v = lax.optimization_barrier(
        (place[:, None], tables, meta, meta_own, meta_other, gain, b_q, b_k, b_v)
    )
    embedded = pl.pallas_call(
        select_kernel,
        out_shape=jax.ShapeDtypeStruct((ROWS, features), jnp.bfloat16),
        compiler_params=pltpu.CompilerParams(vmem_limit_bytes=VMEM),
        cost_estimate=pl.CostEstimate(flops=0, bytes_accessed=14 * 2**20, transcendentals=0),
        name="select",
    )(place, arrived)

    left, right = move(embedded, dx=1), move(embedded, dx=-1)
    across = move(left[:CUT], dx=1), move(right[CUT:], dx=-1)

    def pieces(piece, dx, start=0):
        yield piece, (dx, False, start, piece.shape[0])
        yield move(piece, core=1), (dx, True, start, piece.shape[0])

    pieces_other = [*pieces(left, 3), *pieces(right, 1)]

    kvs, queries, tails = {}, {}, {}
    kv, tails["other"], queries["other"] = project_kv(
        True, meta, slot_map, pieces_other, weights, gain, *tables[1], b_q, b_k, b_v
    )
    kv, *across = lax.optimization_barrier((kv, *across))
    kvs["other"] = [kv] + [move(kv, dz=dz) for dz in (1, 2, 3)]
    pieces_own = [*pieces(embedded, 0), *pieces(across[0], 2), *pieces(across[1], 2, CUT)]
    kv, tails["own"], normed = project_kv(
        False, meta, slot_map, pieces_own, weights, gain, *tables[0], b_q, b_k, b_v
    )
    kvs["own"] = [kv] + [move(kv, dz=dz) for dz in (1, 2, 3)]
    queries["own"] = project_q(slot_map, normed, weights, *tables[0], b_q)
    queries = lax.optimization_barrier(queries)
    every = [kv for pair in zip(kvs["own"], kvs["other"]) for kv in pair]
    theirs = move(attend(meta_other, queries["other"], tails["other"], every), pair=1)
    ours = attend(meta_own, queries["own"], tails["own"], every)
    heads = jnp.where(
        j == 0,
        jnp.concatenate([ours, theirs], axis=1),
        jnp.concatenate([theirs, ours], axis=1),
    )
    return heads[:TOK], heads[TOK : TOK + samples]


def solution(mesh):
    placed = (
        P(("grp", "ctx")),
        P(("grp", "ctx")),
        P("ctx", "tp"),
        P(),
        P(),
        P("ctx", None, "tp"),
        P("ctx", None, "tp"),
        P("ctx", None, "tp"),
        P("tp"),
        P("tp"),
        P("tp"),
    )
    return jax.shard_map(
        local,
        mesh=mesh,
        in_specs=placed,
        out_specs=(P(("grp", "ctx"), "tp"), P(("grp", "ctx"), "tp")),
        check_vma=False,
    )
```

```python
import functools
import math

import jax
import jax.numpy as jnp
from jax import lax
from jax.experimental import pallas as pl
from jax.experimental.pallas import tpu as pltpu
from jax.sharding import PartitionSpec as P

HEAD = 128
EPS = 1e-06
THETA = 1000000.0
NEG = -1e30
AXES = ("ctx", "tp", "grp")
CAP = 128
MSG = 136
ROWS = 528
TOK = 512
SIZE = 4
VMEM = 56 * 1024 * 1024
DEEP = 1280
CUT = 256
WIDE = 256
WIDE = 256
FAR_Z = (3, 1, 2)


def device_number(x, y, z, core):
    return ((z * 2 + x % 2) * 4 + (x // 2) * 2 + core) * 4 + y


def move(array, dx=0, dy=0, dz=0, pair=0, core=0, side=0):
    pairs = []
    for x in range(SIZE):
        for y in range(SIZE):
            for z in range(SIZE):
                for c in range(2):
                    along = (x + dx + side * (2 * (x % 2) - 1)) % SIZE
                    there = along ^ pair, (y + dy) % SIZE, (z + dz) % SIZE, c ^ core
                    pairs.append((device_number(x, y, z, c), device_number(*there)))
    return lax.ppermute(array, AXES, pairs)


def rope_tables(positions):
    half = HEAD // 2
    frequency = jnp.power(THETA, -jnp.arange(half, dtype=jnp.float32) * 2.0 / HEAD)
    angles = positions.astype(jnp.float32)[:, None] * frequency[None, :]
    cosine, sine = jnp.cos(angles), jnp.sin(angles)
    return jnp.concatenate([cosine, cosine], 1), jnp.concatenate([-sine, sine], 1)


def rotate(value, cosine, sine):
    return value * cosine + pltpu.roll(value, HEAD // 2, 1) * sine


def weight_copies(slots, weights, held, sems, low):
    span = pl.ds(low, held.shape[2])
    for bucket in range(16):
        slot = slots[bucket]
        source = weights.at[bucket, :, span]
        pltpu.make_async_copy(source, held.at[slot], sems.at[slot]).start()

    def wait(quarter):
        for slot in range(4 * quarter, 4 * quarter + 4):
            source = weights.at[0, :, span]
            pltpu.make_async_copy(source, held.at[slot], sems.at[slot]).wait()

    return wait


def multiply(k, rows, held, acc):
    product = jnp.dot(
        rows[:, k * DEEP : (k + 1) * DEEP],
        held[4 * k : 4 * k + 4].reshape(DEEP, held.shape[2]),
        preferred_element_type=jnp.float32,
    )
    acc[...] = product if k == 0 else acc[...] + product


def finish_q(acc, b_query, cosine, sine, q_out):
    for head in range(5):
        span = slice(head * HEAD, (head + 1) * HEAD)
        turned = rotate(acc[:, span] + b_query[:, span], cosine[...], sine[...])
        q_out[:, span] = turned.astype(jnp.bfloat16)


def kv_kernel(piece_at, fused, meta, slots, *refs):
    n = len(piece_at)
    weights, gain, cosine, sine, b_query, b_key, b_value = refs[n : n + 7]
    kv_out, tail_out, last_out, rows, held, acc, row_sems, held_sems, out_sem = refs[n + 7 :]
    x, core = meta[0], meta[4]
    low = 5 * HEAD if fused else 0
    copies = []
    for ref, (dx, other, start, count) in zip(refs, piece_at):
        there = lax.rem(x + dx, SIZE)
        feature = 2 * (there // 2) + (1 - core if other else core)
        width = ref.shape[1]
        target = rows.at[pl.ds(start, count), pl.ds(pl.multiple_of(feature * width, 128), width)]
        copies.append(pltpu.make_async_copy(ref, target, row_sems.at[len(copies)]))
    for copy in copies:
        copy.start()
    wait = weight_copies(slots, weights, held, held_sems, 5 * HEAD - low)
    for copy in copies:
        copy.wait()
    step = 48
    lanes = [slice(start, start + HEAD) for start in range(0, rows.shape[1], HEAD)]

    def normalize(index, _):
        span = pl.ds(pl.multiple_of(index * step, 16), step)
        squares = jnp.zeros((step, HEAD), jnp.float32)
        for lane in lanes:
            values = rows[span, lane].astype(jnp.float32)
            squares = squares + values * values
        mean = jnp.sum(squares, axis=-1, keepdims=True) / rows.shape[1]
        factor = lax.rsqrt(mean + EPS)
        for lane in lanes:
            values = rows[span, lane].astype(jnp.float32)
            rows[span, lane] = (values * factor * gain[:, lane]).astype(jnp.bfloat16)
        return 0

    lax.fori_loop(0, ROWS // step, normalize, 0)
    if not fused:
        out = pltpu.make_async_copy(rows, last_out, out_sem)
        out.start()
    for k in range(4):
        wait(k)
        multiply(k, rows, held, acc)
    key = rotate(acc[:, low : low + HEAD] + b_key[...], cosine[...], sine[...])
    value = acc[:, low + HEAD :] + b_value[...]
    kv_out[:TOK] = key[:TOK].astype(jnp.bfloat16)
    tail_out[0] = key[TOK:].astype(jnp.bfloat16)
    tail_out[1] = value[TOK:].astype(jnp.bfloat16)
    for start in range(0, TOK, HEAD):
        kv_out[TOK + start : TOK + start + HEAD] = (
            value[start : start + HEAD].T.astype(jnp.bfloat16)
        )
    if fused:
        finish_q(acc, b_query, cosine, sine, last_out)
    else:
        out.wait()


def q_kernel(
    slots, normed, weights, cosine, sine, b_query, q_out, rows, held, acc, row_sems, held_sems
):
    copies = []
    for k in range(4):
        span = pl.ds(k * DEEP, DEEP)
        copies.append(pltpu.make_async_copy(normed.at[:, span], rows.at[:, span], row_sems.at[k]))
    wait = weight_copies(slots, weights, held, held_sems, 0)
    for copy in copies:
        copy.start()
    for k in range(4):
        wait(k)
        copies[k].wait()
        multiply(k, rows, held, acc)
    finish_q(acc, b_query, cosine, sine, q_out)


SMEM_SPEC = pl.BlockSpec(memory_space=pltpu.SMEM)
VMEM_SPEC = pl.BlockSpec(memory_space=pltpu.VMEM)
ANY_SPEC = pl.BlockSpec(memory_space=pl.ANY)


def project_kv(fused, meta, slots, pieces, weights, gain, cosine, sine, b_q, b_k, b_v):
    width = 4 * DEEP
    columns = 7 * HEAD if fused else 2 * HEAD
    refs, piece_at = zip(*pieces)
    return pl.pallas_call(
        functools.partial(kv_kernel, piece_at, fused),
        out_shape=(
            jax.ShapeDtypeStruct((2 * TOK, HEAD), jnp.bfloat16),
            jax.ShapeDtypeStruct((2, ROWS - TOK, HEAD), jnp.bfloat16),
            jax.ShapeDtypeStruct((ROWS, 5 * HEAD if fused else width), jnp.bfloat16),
        ),
        in_specs=[SMEM_SPEC] * 2 + [ANY_SPEC] * (len(refs) + 1) + [VMEM_SPEC] * 6,
        out_specs=(VMEM_SPEC, VMEM_SPEC, VMEM_SPEC if fused else ANY_SPEC),
        scratch_shapes=[
            pltpu.VMEM((ROWS, width), jnp.bfloat16),
            pltpu.VMEM((16, 320, columns), jnp.bfloat16),
            pltpu.VMEM((ROWS, columns), jnp.float32),
            pltpu.SemaphoreType.DMA((len(refs),)),
            pltpu.SemaphoreType.DMA((16,)),
            pltpu.SemaphoreType.DMA,
        ],
        compiler_params=pltpu.CompilerParams(vmem_limit_bytes=VMEM),
        cost_estimate=pl.CostEstimate(
            flops=2 * ROWS * width * columns, bytes_accessed=30 * 2**20, transcendentals=0
        ),
        name="norm_qkv" if fused else "norm_kv",
    )(meta, slots, *refs, weights, gain, cosine, sine, b_q, b_k, b_v)


def project_q(slots, normed, weights, cosine, sine, b_q):
    width = 4 * DEEP
    return pl.pallas_call(
        q_kernel,
        out_shape=jax.ShapeDtypeStruct((ROWS, 5 * HEAD), jnp.bfloat16),
        in_specs=[SMEM_SPEC] + [ANY_SPEC] * 2 + [VMEM_SPEC] * 3,
        out_specs=VMEM_SPEC,
        scratch_shapes=[
            pltpu.VMEM((ROWS, width), jnp.bfloat16),
            pltpu.VMEM((16, 320, 5 * HEAD), jnp.bfloat16),
            pltpu.VMEM((ROWS, 5 * HEAD), jnp.float32),
            pltpu.SemaphoreType.DMA((4,)),
            pltpu.SemaphoreType.DMA((16,)),
        ],
        compiler_params=pltpu.CompilerParams(vmem_limit_bytes=VMEM),
        cost_estimate=pl.CostEstimate(
            flops=2 * ROWS * width * 5 * HEAD, bytes_accessed=24 * 2**20, transcendentals=0
        ),
        name="query",
    )(slots, normed, weights, cosine, sine, b_q)


def attend_kernel(meta, q, tail, *refs):
    kvs, (out, keys, values, turned, top, total, mixed, sems) = refs[:8], refs[8:]
    z, chunk, j = meta[0], meta[1], meta[2]
    factor = math.log2(math.e) / math.sqrt(HEAD)
    copies = []
    for index, ref in enumerate(kvs):
        place = (1 - j, j)[index] if index < 2 else index
        parts = [(ref.at[pl.ds(0, TOK)], keys.at[pl.ds(place * TOK, TOK)])]
        for low in range(0, TOK, HEAD):
            parts.append(
                (ref.at[pl.ds(TOK + low, HEAD)], values.at[:, pl.ds(place * TOK + low, HEAD)])
            )
        for source, target in parts:
            copies.append(pltpu.make_async_copy(source, target, sems.at[len(copies)]))
    for copy in copies:
        copy.start()
    for head in range(5):
        span = slice(head * HEAD, (head + 1) * HEAD)
        turned[head] = q[:TOK, span].astype(jnp.float32).T.astype(jnp.bfloat16)
    top[...] = jnp.full_like(top, NEG)
    total[...] = jnp.zeros_like(total)
    mixed[...] = jnp.zeros_like(mixed)
    for copy in copies[:10]:
        copy.wait()

    def soften(scores, head, low):
        lanes = slice(low, low + scores.shape[1])
        before = top[head, :, lanes]
        now = jnp.maximum(before, jnp.max(scores, axis=0, keepdims=True))
        scale = jnp.exp2((before - now) * factor)
        expo = jnp.exp2(scores * factor - now * factor)
        top[head, :, lanes] = now
        total[head, :, lanes] = total[head, :, lanes] * scale + jnp.sum(
            expo, axis=0, keepdims=True
        )
        return expo.astype(jnp.bfloat16), scale

    def mix(softened, head, low, there):
        expo, scale = softened
        lanes = slice(low, low + expo.shape[1])
        mixed[head, :, lanes] = mixed[head, :, lanes] * scale + jnp.dot(
            values[:, there], expo, preferred_element_type=jnp.float32
        )

    units = [(head, low) for head in range(5) for low in range(0, TOK, WIDE)]

    def scores_of(head, low, there):
        query = turned[head, :, low : low + WIDE]
        return jnp.dot(keys[there, :], query, preferred_element_type=jnp.float32)

    def fold(start, size, masked=False):
        def there(low):
            return pl.ds(pl.multiple_of(start, TOK), low + WIDE if masked else size)

        ahead = scores_of(*units[0], there(0))
        softened = None
        for index, (head, low) in enumerate(units):
            scores = ahead
            if index + 1 < len(units):
                ahead = scores_of(*units[index + 1], there(units[index + 1][1]))
            if masked:
                key = lax.broadcasted_iota(jnp.int32, scores.shape, 0)
                row = low + lax.broadcasted_iota(jnp.int32, scores.shape, 1)
                scores = jnp.where(key <= row, scores, NEG)
            now = soften(scores, head, low)
            if index > 0:
                mix(softened, *units[index - 1], there(units[index - 1][1]))
            softened = now
        mix(softened, *units[-1], there(units[-1][1]))

    fold((1 - chunk) * TOK, TOK, True)
    for copy in copies[10:]:
        copy.wait()

    @pl.when(chunk == 1)
    def _():
        fold(TOK, TOK)

    @pl.when(z >= 2)
    def _():
        fold(2 * TOK, 4 * TOK)

    @pl.when(lax.rem(z, 2) == 1)
    def _():
        fold(z * 2 * TOK, 2 * TOK)

    for head in range(5):
        span = slice(head * HEAD, (head + 1) * HEAD)
        out[:TOK, span] = (mixed[head] / total[head]).T.astype(jnp.bfloat16)

    size = ROWS - TOK
    blank = jnp.zeros((HEAD - 5 * size, HEAD), jnp.float32)
    query = [
        q[TOK:, head * HEAD : (head + 1) * HEAD].astype(jnp.float32) for head in range(5)
    ]
    query = jnp.concatenate(query + [blank], axis=0)
    own_key, own_value = [
        jnp.concatenate([tail[n].astype(jnp.float32)] * 5 + [blank], axis=0)
        for n in range(2)
    ]
    lanes = slice(0, HEAD)
    own = jnp.sum((query * own_key).T, axis=0, keepdims=True)
    top[0, :, lanes] = own
    total[0, :, lanes] = jnp.ones_like(own)
    mixed[0, :, lanes] = own_value.T
    query = query.T.astype(jnp.bfloat16)

    def visit_all(away, _):
        there = pl.ds(pl.multiple_of(away * 2 * TOK, TOK), 2 * TOK)
        scores = jnp.dot(keys[there, :], query, preferred_element_type=jnp.float32)
        mix(soften(scores, 0, 0), 0, 0, there)
        return 0

    lax.fori_loop(0, SIZE, visit_all, 0)
    done = (mixed[0, :, lanes] / total[0, :, lanes]).T.astype(jnp.bfloat16)
    for head in range(5):
        out[TOK:, head * HEAD : (head + 1) * HEAD] = done[head * size : (head + 1) * size]


def attend(meta, query, tail, kvs):
    return pl.pallas_call(
        attend_kernel,
        out_shape=jax.ShapeDtypeStruct((ROWS, 5 * HEAD), jnp.bfloat16),
        in_specs=[SMEM_SPEC] + [VMEM_SPEC] * 2 + [ANY_SPEC] * 8,
        out_specs=VMEM_SPEC,
        scratch_shapes=[
            pltpu.VMEM((2 * SIZE * TOK, HEAD), jnp.bfloat16),
            pltpu.VMEM((HEAD, 2 * SIZE * TOK), jnp.bfloat16),
            pltpu.VMEM((5, HEAD, TOK), jnp.bfloat16),
            pltpu.VMEM((5, 1, TOK), jnp.float32),
            pltpu.VMEM((5, 1, TOK), jnp.float32),
            pltpu.VMEM((5, HEAD, TOK), jnp.float32),
            pltpu.SemaphoreType.DMA((40,)),
        ],
        compiler_params=pltpu.CompilerParams(vmem_limit_bytes=VMEM),
        cost_estimate=pl.CostEstimate(
            flops=0, bytes_accessed=60 * 2**20, transcendentals=0
        ),
        name="attend",
    )(meta, query, tail, *kvs)


def select_kernel(place, arrived, out, held, spread, sem):
    copy = pltpu.make_async_copy(arrived, held, sem)
    copy.start()
    found = place[...] == lax.broadcasted_iota(jnp.int32, spread.shape, 1)
    spread[...] = found.astype(jnp.bfloat16)
    copy.wait()
    out[...] = jnp.dot(
        spread[...], held[...], preferred_element_type=jnp.float32
    ).astype(jnp.bfloat16)


def nought(array, limit):
    held = lax.optimization_barrier(array)[(0,) * array.ndim]
    return (held > limit).astype(jnp.int32)


def counts_before(flags):
    upto = jnp.arange(TOK)[:, None] <= jnp.arange(TOK)[None, :]
    return jnp.dot(
        flags.astype(jnp.bfloat16), upto.astype(jnp.bfloat16), preferred_element_type=jnp.float32
    ).astype(jnp.int32)


def local(
    prompt_ids,
    first_ids,
    table,
    norm_gain,
    slot_map,
    w_query,
    key_weight,
    value_weight,
    b_query,
    b_key,
    value_bias,
):
    ctx = lax.axis_index("ctx")
    tp = lax.axis_index("tp")
    y = lax.axis_index("grp")
    z, j = ctx // 2, ctx % 2
    x, core = (tp // 2) * 2 + j, tp % 2
    vocab_dev, features = table.shape
    samples = first_ids.shape[0]

    def columns(head):
        pick = lambda w, n: lax.dynamic_slice_in_dim(w, head * n, n, 2)
        return jnp.concatenate(
            [pick(w_query, 5 * HEAD), pick(key_weight, HEAD), pick(value_weight, HEAD)], axis=2
        )

    mine = jnp.concatenate([prompt_ids, first_ids])[None]
    both = jnp.concatenate([mine, move(mine, side=1)], axis=0)
    ids = jnp.concatenate([both, move(both, dz=-1), move(both, dz=2), move(both, dz=1)], axis=0)

    own = columns(j)
    give = columns(1 - j)
    first = y % 2
    near0 = move(lax.dynamic_index_in_dim(give, first, 0, keepdims=False), pair=1)

    wanted = ids - ctx * vocab_dev
    inside = (wanted >= 0) & (wanted < vocab_dev)
    rank = jnp.where(inside[:, :TOK], counts_before(inside[:, :TOK]) - 1, -1)
    at_slot = rank[:, None, :] == jnp.arange(CAP, dtype=jnp.int32)[None, :, None]
    chosen = jnp.sum(jnp.where(at_slot, wanted[:, None, :TOK], 0), axis=-1)
    chosen = jnp.concatenate(
        [
            chosen,
            jnp.where(inside[:, TOK:], wanted[:, TOK:], 0),
            jnp.zeros((8, MSG - CAP - samples), jnp.int32),
        ],
        axis=1,
    )
    chunks = jnp.arange(2 * SIZE, dtype=jnp.int32)
    lies = ((chunks // 2 - z) % SIZE) * 2 + (chunks + j) % 2
    chosen = jnp.sum(jnp.where((lies[:, None] == chunks)[:, :, None], chosen[None], 0), axis=1)
    wait_ids = nought(chosen, 1 << 30)
    part = jnp.where(
        j + wait_ids == y // 2, lax.dynamic_index_in_dim(own, first, 0, keepdims=False), near0
    )
    same_j = [[(2 * n + k) * SIZE + m for n in range(SIZE) for m in range(SIZE)] for k in (0, 1)]
    weights = lax.all_gather(
        part, ("ctx", "grp"), axis_index_groups=same_j, axis=0, tiled=False
    )
    chosen = chosen + nought(part, 1000)
    message = table.at[chosen.reshape(-1)].get(mode="promise_in_bounds")
    arrived = lax.all_to_all(message, "ctx", 0, 0, tiled=True)

    wait_message = nought(message, 1000)
    owner = (mine[0] + wait_message) // vocab_dev
    held_by = owner[None, :TOK] == chunks[:, None]
    place = jnp.sum(jnp.where(held_by, counts_before(held_by) - 1, 0), axis=0)
    place = jnp.concatenate([place, CAP + jnp.arange(samples, dtype=jnp.int32)]) + owner * MSG
    place = jnp.concatenate([place, jnp.full((ROWS - TOK - samples,), -1, jnp.int32)])
    positions = jnp.arange(ROWS, dtype=jnp.int32) + wait_message
    tables = [
        rope_tables(jnp.where(positions < TOK, (2 * z + n) * TOK + positions, SIZE * 2 * TOK))
        for n in (j, 1 - j)
    ]
    meta = jnp.stack([x, z, y, j, core]).astype(jnp.int32)
    meta_own = jnp.stack([z, j, j]).astype(jnp.int32)
    meta_other = jnp.stack([z, 1 - j, j]).astype(jnp.int32)
    take = lambda vector, n: lax.dynamic_slice_in_dim(vector, j * n, n, 0)[None]
    gain, b_q, b_k, b_v = (
        norm_gain[None], take(b_query, 5 * HEAD), take(b_key, HEAD), take(value_bias, HEAD)
    )
    place, tables, meta, meta_own, meta_other, gain, b_q, b_k, b_v = lax.optimization_barrier(
        (place[:, None], tables, meta, meta_own, meta_other, gain, b_q, b_k, b_v)
    )
    embedded = pl.pallas_call(
        select_kernel,
        out_shape=jax.ShapeDtypeStruct((ROWS, features), jnp.bfloat16),
        in_specs=[VMEM_SPEC, ANY_SPEC],
        out_specs=VMEM_SPEC,
        scratch_shapes=[
            pltpu.VMEM(arrived.shape, jnp.bfloat16),
            pltpu.VMEM((ROWS, arrived.shape[0]), jnp.bfloat16),
            pltpu.SemaphoreType.DMA,
        ],
        compiler_params=pltpu.CompilerParams(vmem_limit_bytes=VMEM),
        cost_estimate=pl.CostEstimate(flops=0, bytes_accessed=14 * 2**20, transcendentals=0),
        name="select",
    )(place, arrived)

    left, right = move(embedded, dx=1), move(embedded, dx=-1)
    across = move(left[:CUT], dx=1), move(right[CUT:], dx=-1)

    def pieces(piece, dx, start=0):
        yield piece, (dx, False, start, piece.shape[0])
        yield move(piece, core=1), (dx, True, start, piece.shape[0])

    pieces_other = [*pieces(left, 3), *pieces(right, 1)]

    kvs, queries, tails = {}, {}, {}
    kv, tails["other"], queries["other"] = project_kv(
        True, meta, slot_map, pieces_other, weights, gain, *tables[1], b_q, b_k, b_v
    )
    kv, *across = lax.optimization_barrier((kv, *across))
    kvs["other"] = [kv] + [move(kv, dz=dz) for dz in (1, 2, 3)]
    pieces_own = [*pieces(embedded, 0), *pieces(across[0], 2), *pieces(across[1], 2, CUT)]
    kv, tails["own"], normed = project_kv(
        False, meta, slot_map, pieces_own, weights, gain, *tables[0], b_q, b_k, b_v
    )
    kvs["own"] = [kv] + [move(kv, dz=dz) for dz in (1, 2, 3)]
    queries["own"] = project_q(slot_map, normed, weights, *tables[0], b_q)
    queries = lax.optimization_barrier(queries)
    every = [kv for pair in zip(kvs["own"], kvs["other"]) for kv in pair]
    theirs = move(attend(meta_other, queries["other"], tails["other"], every), pair=1)
    ours = attend(meta_own, queries["own"], tails["own"], every)
    def beside(low, high):
        mine, other = ours[low:high], theirs[low:high]
        return jnp.where(
            j == 0,
            jnp.concatenate([mine, other], axis=1),
            jnp.concatenate([other, mine], axis=1),
        )

    return beside(0, TOK), beside(TOK, TOK + samples)


def solution(mesh):
    placed = (
        P(("grp", "ctx")),
        P(("grp", "ctx")),
        P("ctx", "tp"),
        P(),
        P(),
        P("ctx", None, "tp"),
        P("ctx", None, "tp"),
        P("ctx", None, "tp"),
        P("tp"),
        P("tp"),
        P("tp"),
    )
    return jax.shard_map(
        local,
        mesh=mesh,
        in_specs=placed,
        out_specs=(P(("grp", "ctx"), "tp"), P(("grp", "ctx"), "tp")),
        check_vma=False,
    )
```
